512 devices in a mesh: lon: 32 (over x, y), lat: 16 (over z, core).
Axes of the slice: x: 4, y: 8, z: 8, core: 2. Of those that a mesh axis runs over, the one named last changes fastest.
Arguments:
- spectra: bfloat16 [2, 33, 128, 20480], P(None, None, 'lat', 'lon'), may hold values from 0.049804688 to 1
- supersat: bfloat16 [2, 128, 20480], P(None, 'lat', 'lon'), may hold values from -3 to 3
- cloud_flags: int32 [20480], P('lon'), may hold values from 0 to 1, as said below
- pair_kernel: bfloat16 [33, 33, 33], replicated, may hold values from -0.1875 to 0.1875
- rime_kernel: bfloat16 [33, 33, 33], replicated, may hold values from -0.1875 to 0.1875
- growth_matrix: bfloat16 [2, 33, 33], replicated, may hold values from -1 to 1
- fall_speed: float32 [2, 33], replicated, may hold values from 0.3 to 30
- density_factor: float32 [128], replicated, may hold values from 0.5 to 2
Outputs:
- tendency: bfloat16 [2, 33, 128, 20480], P(None, None, 'lat', 'lon')
The draws below stay inside these ranges and needn't reach their ends.
Inputs may be any that keep to these rules, and one draw needn't show every extreme that they name: `cloud_flags`: 1 marks a column that takes part in collisions, 0 a clear one.
All inputs are finite; a program needn't handle non-finite values.
Results may differ from the reference program's by a relative error of at most 0.005.
Values may be sent and summed in bfloat16 or wider, within the bound.
No kernel may reach another device: no remote copies, remote signals or barrier semaphores. Data moves between devices by JAX's collectives and lax.ppermute only.
A program may use at most 128 MiB of HBM per device.

```python
import math
import jax
import jax.numpy as jnp
from jax import lax

BINS = 33
LEV = 128
COL_DEV = 40
ITERS = 2
COLS = 20480


def draw_cloud_flags(key, part):
    key = jax.random.fold_in(key, 11)
    level_key, pick_key = jax.random.split(key)
    coverage = jax.random.randint(level_key, (COLS // COL_DEV,), 5, 96)
    coverage = jnp.repeat(coverage, COL_DEV)
    dice_rolls = jax.random.randint(pick_key, (COLS,), 0, 100)
    return (dice_rolls < coverage).astype(jnp.int32)


def shard_levels(rng, shape, pieces, low, top_value):
    def one(dim, shards_of):
        heights = jax.random.uniform(jax.random.fold_in(jax.random.fold_in(rng, 6), dim), (shards_of,), jnp.float32, low / len(pieces), top_value / len(pieces))
        return jnp.repeat(jnp.exp(heights), shape[dim] // shards_of).reshape((-1,) + (1,) * (len(shape) - dim - 1))

    factor_of = one(*pieces[0])
    for cut in pieces[1:]:
        factor_of = factor_of * one(*cut)
    return factor_of


def normal_values(stream_key, shape, scale, reach, cuts=(), held_as=jnp.bfloat16):
    entries = jax.random.normal(stream_key, shape, jnp.float32) * scale
    if len(cuts) > 0:
        entries = shard_levels(stream_key, shape, cuts, -0.22, 0.18) * entries
    return jnp.clip(entries, min=-reach, max=reach).astype(held_as)


def setup_inputs(seed: int = 0) -> dict:
    seeds = jax.random.split(jax.random.key(seed), 9)
    return {
        "spectra": jnp.clip(jnp.exp(math.log(1.0) - 2.9996462 * jax.random.uniform(seeds[0], (2, BINS, LEV, COLS), jnp.float32) ** shard_levels(seeds[0], (2, BINS, LEV, COLS), ((2, 16), (3, 32)), -0.2, 0.2)), 0.049804688, 1.0).astype(jnp.bfloat16),
        "supersat": normal_values(seeds[1], (2, LEV, COLS), 0.5, 3.0, ((1, 16), (2, 32))),
        "cloud_flags": draw_cloud_flags(jax.random.fold_in(seeds[8], 71), 0),
        "pair_kernel": normal_values(seeds[3], (BINS, BINS, BINS), (BINS * BINS) ** -0.5, 0.1875),
        "rime_kernel": normal_values(seeds[4], (BINS, BINS, BINS), (BINS * BINS) ** -0.5, 0.1875),
        "growth_matrix": normal_values(seeds[5], (2, BINS, BINS), BINS ** -0.5, 1.0),
        "fall_speed": jnp.clip(jnp.exp(jax.random.uniform(seeds[6], (2, BINS), jnp.float32, math.log(0.3), math.log(30.0))), 0.3, 30.0),
        "density_factor": jnp.clip(jnp.exp(jax.random.uniform(seeds[7], (LEV,), jnp.float32, math.log(0.5), math.log(2.0))), 0.5, 2.0),
    }


time_step = 1.0


def settling_matrix(fall_speed, density_factor):
    courant = time_step * fall_speed.reshape(-1)[:, None] * density_factor[None, :]
    ratios = courant[:, :-1] / (1.0 + courant[:, 1:])
    log_sums = jnp.concatenate([jnp.zeros((courant.shape[0], 1), jnp.float32), jnp.cumsum(jnp.log(ratios), axis=1)], axis=1)
    level_index = jnp.arange(courant.shape[1], dtype=jnp.int32)
    below_mask = level_index[:, None] >= level_index[None, :]
    spread = jnp.where(below_mask[None], log_sums[:, :, None] - log_sums[:, None, :], 0.0)
    return jnp.where(below_mask[None], jnp.exp(spread), 0.0) / (1.0 + courant[:, None, :])


def pair_gains(col_block, pair_kernel, rime_kernel):
    bin_count = pair_kernel.shape[0]
    flat_rows = col_block.reshape(2 * bin_count, -1)
    liquid = flat_rows[:bin_count]
    frozen = flat_rows[bin_count:]
    pair_terms = jnp.dot(pair_kernel.reshape(bin_count * bin_count, bin_count), liquid, preferred_element_type=jnp.float32)
    pair_terms = pair_terms.astype(jnp.bfloat16).reshape(bin_count, bin_count, -1)
    rime_terms = jnp.dot(rime_kernel.reshape(bin_count * bin_count, bin_count), frozen, preferred_element_type=jnp.float32)
    rime_terms = rime_terms.astype(jnp.bfloat16).reshape(bin_count, bin_count, -1)
    liquid_wide = liquid.astype(jnp.float32)
    liquid_gain = jnp.einsum('kir,ir->kr', pair_terms.astype(jnp.float32), liquid_wide)
    frozen_gain = jnp.einsum('kir,ir->kr', rime_terms.astype(jnp.float32), liquid_wide)
    return jnp.concatenate([liquid_gain, frozen_gain], axis=0).reshape(col_block.shape)


def reference(spectra, supersat, cloud_flags, pair_kernel, rime_kernel, growth_matrix, fall_speed, density_factor):
    channels = 2 * BINS
    initial = jnp.transpose(spectra.astype(jnp.float32), (0, 1, 3, 2)).reshape(channels, COLS, LEV)
    saturation = jnp.transpose(supersat.astype(jnp.float32), (0, 2, 1))
    cloudy = cloud_flags.astype(jnp.float32)
    settle = settling_matrix(fall_speed, density_factor)
    block_width = math.gcd(COLS, 64)
    block_count = COLS // block_width
    spectrum = initial
    for substep in range(ITERS):
        rounded = spectrum.astype(jnp.bfloat16)
        blocks = jnp.transpose(rounded.reshape(channels, block_count, block_width, LEV), (1, 0, 2, 3))
        gathered = lax.map(lambda col_block: pair_gains(col_block, pair_kernel, rime_kernel), blocks)
        collided = jnp.transpose(gathered, (1, 0, 2, 3)).reshape(channels, COLS, LEV) * cloudy[None, :, None]
        growth = jnp.einsum('skj,sjcl->skcl', growth_matrix.astype(jnp.float32), rounded.reshape(2, BINS, COLS, LEV).astype(jnp.float32))
        growth = growth * saturation[:, None]
        spectrum = spectrum + time_step * (collided + growth.reshape(channels, COLS, LEV))
        spectrum = jnp.einsum('blm,bcm->bcl', settle, spectrum, precision=lax.Precision.HIGHEST)
    tendency = (spectrum - initial) / (ITERS * time_step)
    return jnp.transpose(tendency.astype(jnp.bfloat16).reshape(2, BINS, COLS, LEV), (0, 1, 3, 2))
```

```python
import functools

import jax
import jax.numpy as jnp
from jax import lax
from jax.experimental import pallas as pl
from jax.experimental.pallas import tpu as pltpu
from jax.sharding import PartitionSpec as P

BINS = 33
HALF = 40
ROWS = 2 * HALF
SLAB = 8
COLS = 640
LANES = 128
MINE = 3 * LANES
SENT = BINS + 1
UNITS = 5
CHIPS = 8
GROUP = 3
DEVS = 2 * CHIPS
FLAT = 168
DEPTH = 11
F32 = jnp.float32
BF16 = jnp.bfloat16

VMEM = pl.BlockSpec(memory_space=pltpu.VMEM)
SMEM = pl.BlockSpec(memory_space=pltpu.SMEM)
HBM = pl.BlockSpec(memory_space=pltpu.HBM)
PARAMS = pltpu.CompilerParams(vmem_limit_bytes=24 * 1024 * 1024)


def on_left():
    return lax.broadcasted_iota(jnp.int32, (1, LANES), 1) < LANES // 2


def turned(value):
    return pltpu.roll(value, LANES // 2, 1)


def padded(value, rows, lanes):
    have_rows, have_lanes = value.shape
    if lanes > have_lanes:
        value = jnp.concatenate([value, jnp.zeros((have_rows, lanes - have_lanes), value.dtype)], axis=1)
    if rows > have_rows:
        value = jnp.concatenate([value, jnp.zeros((rows - have_rows, lanes), value.dtype)], axis=0)
    return value


def fall_column(fall_ref):
    row = lax.broadcasted_iota(jnp.int32, (HALF, BINS), 0)
    lane = lax.broadcasted_iota(jnp.int32, (HALF, BINS), 1)
    parts = []
    for s in range(2):
        spread = jnp.broadcast_to(fall_ref[s : s + 1, :], (HALF, BINS))
        parts.append(jnp.sum(jnp.where(row == lane, spread, 0.0), axis=1, keepdims=True))
    return jnp.concatenate(parts, axis=0)


def lane_of(value, lane):
    return jnp.broadcast_to(value[:, lane : lane + 1], (ROWS, LANES))


def settle_tables(courant, chip, courant_ref, inverse_ref, lower_ref):
    own = pltpu.roll(courant, lax.rem(LANES - 2 * SLAB * chip, LANES), 1)
    left = on_left()
    lower = None
    for l in range(2 * SLAB):
        here = lane_of(own, l)
        inverse = 1.0 / (1.0 + here)
        lower = None if l < SLAB else inverse if l == SLAB else lower * last * inverse
        last = here
        courant_ref[l] = here
        inverse_ref[l] = inverse
        if l >= SLAB:
            at = l - SLAB
            courant_ref[l + SLAB] = jnp.where(left, courant_ref[at], here)
            inverse_ref[l + SLAB] = jnp.where(left, inverse_ref[at], inverse)
            lower_ref[at] = jnp.where(left, 0.0, lower)
    lower_ref[SLAB] = jnp.where(left, 0.0, lower * last)


def arrive_table(courant_ref, inverse_ref, arrive_ref):
    left = on_left()
    arrive = inverse_ref[0]
    for l in range(2 * SLAB):
        if l > 0:
            arrive = arrive * courant_ref[l - 1] * inverse_ref[l]
        arrive_ref[l] = arrive
        if l >= SLAB:
            arrive_ref[l + SLAB] = jnp.where(left, arrive_ref[l - SLAB], arrive)


def flat_of(a, b, packed):
    middle = jnp.where(on_left(), turned(packed[HALF:]), packed[:HALF])
    pieces = (a[:HALF], a[HALF:], b[:HALF], b[HALF:], middle)
    row = lax.broadcasted_iota(jnp.int32, (8, LANES), 0)
    rest = jnp.zeros((8, LANES), F32)
    for at, piece in enumerate(pieces):
        tail = piece[32:]
        rest = jnp.where(row == at, tail if at == 0 else pltpu.roll(tail, at, 0), rest)
    return jnp.concatenate([piece[:32] for piece in pieces] + [rest], axis=0)


def from_flat(flat):
    row = lax.broadcasted_iota(jnp.int32, (8, LANES), 0)
    rest = flat[160:]
    pieces = []
    for at in range(5):
        tail = rest if at == 0 else pltpu.roll(rest, 8 - at, 0)
        pieces.append(jnp.concatenate([flat[32 * at : 32 * (at + 1)], jnp.where(row == 0, tail, 0.0)], axis=0))
    return pieces


def scan_weights(courant, chip, factor_ref, weight_ref):
    ratio = courant / (1.0 + courant)
    for step in (1, 2, 4, 8):
        ratio = ratio * pltpu.roll(ratio, LANES - step, 1)
    for e in range(CHIPS):
        factor_ref[e] = lane_of(ratio, 2 * SLAB * e)
    one = jnp.ones((ROWS, LANES), F32)

    def product(first, end):
        return lax.fori_loop(first, end, lambda e, w: w * factor_ref[e], one)

    place = chip % GROUP
    first = chip - place
    size = jnp.minimum(GROUP, CHIPS - first)
    for r in range(GROUP):
        there = jnp.where(place >= r, place - r, place - r + size)
        fits = there >= 0
        if r > 0:
            w = jnp.where(fits & (there < place), product(first + there + 1, chip), 0.0)
            weight_ref[r - 1] = flat_of(w, w, w)
        w = jnp.where(fits, product(first + there + 1, first + size), 0.0)
        weight_ref[2 + r] = flat_of(w, w, w)
    for back in range(1, GROUP):
        start = first - GROUP * (back - 1)
        w = jnp.where(first >= GROUP * back, product(jnp.maximum(start, 0), chip), 0.0)
        weight_ref[4 + back] = flat_of(w, w, w)


def pack_weights(pair_ref, rime_ref, growth_ref, wide_ref, slim_ref, main_ref, rest_ref):
    for k in range(BINS):
        slim_ref[2 * k : 2 * k + 2, :] = padded(growth_ref[k].astype(F32), 2, LANES)
    for at, source in ((0, pair_ref), (1, rime_ref)):
        for k in range(BINS - 1):
            wide_ref[HALF * k : HALF * (k + 1), :] = padded(source[k].astype(F32), HALF, LANES)
        for i in range(BINS):
            main_ref[i, 32 * at : 32 * (at + 1), :] = wide_ref[pl.ds(i, 32, stride=HALF), :].astype(BF16)
        rest_ref[0, 48 * at : 48 * (at + 1), :] = padded(source[BINS - 1].astype(F32), 48, LANES).astype(BF16)
        grow = slim_ref[pl.ds(at, BINS, stride=2), :]
        rest_ref[1, 48 * at : 48 * (at + 1), :] = padded(grow, 48, LANES).astype(BF16)


def two_sided(block):
    half = block.shape[0] // 2
    empty = jnp.zeros((half, LANES), block.dtype)
    return jnp.concatenate(
        [
            jnp.concatenate([block[:half], empty], axis=1),
            jnp.concatenate([empty, block[half:]], axis=1),
        ],
        axis=0,
    )


def substep(round_ref, base_ref, state_ref, sat_ref, flag_ref, main_ref, rest_ref):
    steps = 2 * UNITS

    def place(step):
        block, first = step // 2, (step % 2) * 4
        return block, [(first + 2 * m, first + 2 * m + 1) for m in range(2)]

    def wide(ref, spot, rows, m):
        block, levels = spot
        return jnp.concatenate([ref[block, l, rows, :] for l in levels[m]], axis=1)

    def scoped(*accs):
        accs = (accs[: DEPTH + 2], accs[DEPTH + 2 :])

        def push(spot):
            empty = jnp.zeros((LANES - 48, 2 * LANES), BF16)
            for m in range(2):
                liquid = padded(wide(round_ref, spot, slice(0, HALF), m), 48, 2 * LANES).astype(BF16)
                frozen = padded(wide(round_ref, spot, slice(HALF, ROWS), m), 48, 2 * LANES).astype(BF16)
                pltpu.matmul_push_rhs(jnp.concatenate([liquid, empty, frozen, empty], axis=0), 0, m)

        def issue(j):
            lhs = two_sided(main_ref[j] if j < BINS else rest_ref[j - BINS])
            for m in range(2):
                acc = accs[m][j % DEPTH] if j < BINS else accs[m][DEPTH + j - BINS]
                pltpu.matmul_acc_lhs(acc, lhs, load_staged_rhs=0 if j == 0 else None)

        def body(step, carry):
            spot = place(step)
            block, levels = spot
            after = place(jnp.minimum(step + 1, steps - 1))
            sums = [jnp.zeros((64, 2 * LANES), F32) for m in range(2)]
            for i in range(BINS):
                if i == DEPTH - 1:
                    push(after)
                for m in range(2):
                    term = pltpu.matmul_pop(accs[m][i % DEPTH])
                    sums[m] = sums[m] + term * wide(round_ref, spot, slice(i, i + 1), m)
                if i + DEPTH < BINS:
                    issue(i + DEPTH)
                else:
                    if i + DEPTH == BINS:
                        issue(BINS)
                        issue(BINS + 1)
                    issue(i + DEPTH - BINS)
            flag = flag_ref[block]
            flag = jnp.concatenate([flag, flag], axis=1)
            for m in range(2):
                last = pltpu.matmul_pop(accs[m][DEPTH])
                grow = pltpu.matmul_pop(accs[m][DEPTH + 1])
                liquid = wide(round_ref, spot, slice(0, HALF), m)
                for s in range(2):
                    tail = jnp.sum(last[48 * s : 48 * s + HALF] * liquid, axis=0, keepdims=True)
                    tail = padded(tail, 8, 2 * LANES)
                    gain = jnp.concatenate([sums[m][32 * s : 32 * (s + 1)], tail], axis=0) * flag
                    sat = jnp.concatenate([sat_ref[block, s * SLAB + l] for l in levels[m]], axis=1)
                    gain = gain + grow[48 * s : 48 * s + HALF] * sat
                    for half, l in enumerate(levels[m]):
                        rows = slice(HALF * s, HALF * (s + 1))
                        part = gain[:, half * LANES : (half + 1) * LANES]
                        state_ref[block, l, rows, :] = base_ref[block, l, rows, :] + part
            return carry

        push(place(0))
        for j in range(DEPTH):
            issue(j)
        lax.fori_loop(0, steps, body, 0)
        for j in range(DEPTH):
            for m in range(2):
                pltpu.matmul_pop(accs[m][j])

    pl.run_scoped(scoped, *accumulators())


def settle(state_ref, courant_ref, inverse_ref, lower_ref, flux_ref):
    def column(units, first, levels):
        flux = None
        for at in range(levels):
            u, l = units[at // SLAB], at % SLAB
            state = state_ref[u, l] if flux is None else state_ref[u, l] + flux
            settled = state * inverse_ref[first + at]
            state_ref[u, l] = settled
            flux = courant_ref[first + at] * settled
        return flux

    a = column((0, 1), 0, 2 * SLAB)
    b = column((2, 3), 0, 2 * SLAB)
    packed = column((4,), 2 * SLAB, SLAB)
    upper = turned(packed)
    for l in range(SLAB):
        state_ref[4, l] = state_ref[4, l] + lower_ref[l] * upper
    packed = packed + lower_ref[SLAB] * upper
    flux_ref[...] = flat_of(a, b, packed).astype(BF16)


def arrivals(prefix_ref, far_ref, near_ref, weight_ref):
    flux = prefix_ref[...] + weight_ref[5] * near_ref[...].astype(F32) + weight_ref[6] * far_ref[...].astype(F32)
    pieces = from_flat(flux)
    middle = pieces[4]
    other = turned(middle)
    left = on_left()
    packed = [jnp.where(left, other, middle), jnp.where(left, middle, other)]
    return tuple(jnp.concatenate(x, axis=0) for x in (pieces[0:2], pieces[2:4], packed))


def with_arrivals(state_ref, arrive_ref, fluxes, put):
    for u in range(UNITS):
        for l in range(SLAB):
            level = (l, SLAB + l, l, SLAB + l, 2 * SLAB + l)[u]
            put(u, l, state_ref[u, l] + arrive_ref[level] * fluxes[u // 2])


def table_kernel(
    index_ref, pair_ref, rime_ref, growth_ref, fall_ref, dens_ref,
    main_ref, rest_ref, courant_ref, inverse_ref, lower_ref,
    wide_ref, slim_ref,
):
    chip = index_ref[0] // 2
    courant = fall_column(fall_ref) * dens_ref[...]
    settle_tables(courant, chip, courant_ref, inverse_ref, lower_ref)
    pack_weights(pair_ref, rime_ref, growth_ref, wide_ref, slim_ref, main_ref, rest_ref)


def weight_kernel(index_ref, fall_ref, dens_ref, courant_ref, inverse_ref, flux_ref, arrive_ref, weight_ref, factor_ref):
    courant = fall_column(fall_ref) * dens_ref[...]
    arrive_table(courant_ref, inverse_ref, arrive_ref)
    scan_weights(courant, index_ref[0] // 2, factor_ref, weight_ref)


def load_kernel(
    index_ref, spectra_hbm, sat_hbm, flag_hbm, pair_hbm, rime_hbm, growth_hbm, fall_hbm, dens_hbm,
    sent_ref, own_ref, flag_ref, pair_ref, rime_ref, growth_ref, fall_ref, dens_ref,
    sems,
):
    core = index_ref[0] % 2
    pieces = []
    for at, ref in ((1 - core, sent_ref), (core, own_ref)):
        cols = pl.ds(pl.multiple_of(at * 2 * LANES, LANES), MINE)
        pieces.append((spectra_hbm.at[:, :, :, cols], ref.at[:, pl.ds(0, BINS)]))
        pieces.append((sat_hbm.at[:, :, cols], ref.at[:, BINS]))
    pieces += [(fall_hbm, fall_ref), (dens_hbm, dens_ref), (pair_hbm, pair_ref), (rime_hbm, rime_ref)]
    pieces += [(growth_hbm, growth_ref), (flag_hbm, flag_ref)]
    copies = [pltpu.make_async_copy(a, b, sems.at[n]) for n, (a, b) in enumerate(pieces)]
    for copy in copies:
        copy.start()
    for copy in copies:
        copy.wait()


def first_kernel(
    index_ref, own_ref, flag_row_ref, other_ref,
    main_ref, rest_ref, courant_ref, inverse_ref, lower_ref,
    state_ref, flux_ref, initial_ref, sat_ref, flag_ref,
):
    core = index_ref[0] % 2
    for u in range(UNITS):
        for l in range(SLAB):
            for s in range(2):
                row = u * SLAB * ROWS + ROWS * l + HALF * s + 32
                initial_ref[row : row + 8, :] = jnp.zeros((8, LANES), F32)
    a, b, middle = (pl.ds(pl.multiple_of(at * LANES, LANES), LANES) for at in (core, core + 1, 2 - 2 * core))
    first = core == 0
    own_half = on_left() == first

    def in_units(s, n):
        units = []
        for cols in (a, b):
            own, other = own_ref[s, n, :, cols].astype(F32), other_ref[s, n, :, cols].astype(F32)
            units += [jnp.where(first, own, other), jnp.where(first, other, own)]
        own, other = own_ref[s, n, :, middle].astype(F32), other_ref[s, n, :, middle].astype(F32)
        return units + [jnp.where(own_half, own, turned(other))]

    flags = (flag_row_ref[...] != 0).astype(F32)
    row_a, row_b = (jnp.where(first, flags[i : i + 1], flags[i + 3 : i + 4]) for i in range(2))
    flag_units = row_a, row_a, row_b, row_b, jnp.where(own_half, flags, turned(flags))[2:3]
    for u in range(UNITS):
        flag_ref[u] = flag_units[u]
    for s in range(2):
        units = in_units(s, BINS)
        for u in range(UNITS):
            for l in range(SLAB):
                sat_ref[u, s * SLAB + l] = units[u][l : l + 1]
        for n in range(BINS):
            units = in_units(s, n)
            for u in range(UNITS):
                initial_ref[pl.ds(u * SLAB * ROWS + HALF * s + n, SLAB, stride=ROWS), :] = units[u]
    initial = initial_ref.reshape(UNITS, SLAB, ROWS, LANES)
    substep(initial, initial, state_ref, sat_ref, flag_ref, main_ref, rest_ref)
    settle(state_ref, courant_ref, inverse_ref, lower_ref, flux_ref)


def second_kernel(
    state_in, prefix_ref, far_ref, near_ref, weight_ref, sat_ref, flag_ref, main_ref, rest_ref,
    courant_ref, inverse_ref, arrive_ref, lower_ref,
    state_ref, flux_ref,
    round_ref,
):
    def put(u, l, state):
        state_ref[u, l] = state
        round_ref[u, l] = state.astype(BF16).astype(F32)

    with_arrivals(state_in, arrive_ref, arrivals(prefix_ref, far_ref, near_ref, weight_ref), put)
    substep(round_ref, state_ref, state_ref, sat_ref, flag_ref, main_ref, rest_ref)
    settle(state_ref, courant_ref, inverse_ref, lower_ref, flux_ref)


def group_kernel(flux_ref, got1_ref, got2_ref, weight_ref, prefix_ref, send_ref):
    got1, got2 = got1_ref[...].astype(F32), got2_ref[...].astype(F32)
    prefix_ref[...] = weight_ref[0] * got1 + weight_ref[1] * got2
    total = weight_ref[2] * flux_ref[...].astype(F32) + weight_ref[3] * got1 + weight_ref[4] * got2
    send_ref[...] = total.astype(BF16)


def last_kernel(
    of_own, index_ref, state_ref, initial_ref, prefix_ref, far_ref, near_ref, weight_ref, arrive_ref,
    part_ref,
    change_ref,
):
    core = index_ref[0] % 2
    slab = core if of_own else 1 - core
    fluxes = arrivals(prefix_ref, far_ref, near_ref, weight_ref)
    for k in range(3):
        u = 2 * k + slab if k < 2 else 4
        for l in range(SLAB):
            level = SLAB * slab + l if k < 2 else 2 * SLAB + l
            row = u * SLAB * ROWS + ROWS * l
            state = state_ref[u, l] + arrive_ref[level] * fluxes[k]
            start = initial_ref[pl.ds(pl.multiple_of(row, 8), ROWS), :]
            change_ref[(k * SLAB + l) * ROWS : (k * SLAB + l + 1) * ROWS, :] = (state - start) * 0.5
    spots = [pl.ds(pl.multiple_of(at * LANES, LANES), LANES) for at in (core, core + 1, 2 - 2 * core)]
    for s in range(2):
        for n in range(BINS):
            for k in range(3):
                rows = change_ref[pl.ds(k * SLAB * ROWS + HALF * s + n, SLAB, stride=ROWS), :]
                if k == 2 and not of_own:
                    rows = turned(rows)
                part_ref[s, n, :, spots[k]] = rows.astype(BF16)


def merge_kernel(index_ref, keep_ref, got_ref, out_hbm, middle_ref, sems):
    core = index_ref[0] % 2

    def merge(left_ref, right_ref):
        parts = [
            (left_ref.at[:, :, :, pl.ds(0, 2 * LANES)], out_hbm.at[:, :, :, pl.ds(0, 2 * LANES)]),
            (right_ref.at[:, :, :, pl.ds(LANES, 2 * LANES)], out_hbm.at[:, :, :, pl.ds(3 * LANES, 2 * LANES)]),
            (middle_ref, out_hbm.at[:, :, :, pl.ds(2 * LANES, LANES)]),
        ]
        copies = [pltpu.make_async_copy(x, y, sems.at[n]) for n, (x, y) in enumerate(parts)]
        copies[0].start()
        copies[1].start()
        side = lax.broadcasted_iota(jnp.int32, (2, BINS, SLAB, LANES), 3) < LANES // 2
        middle_ref[...] = jnp.where(
            side, left_ref[:, :, :, 2 * LANES :].astype(F32), right_ref[:, :, :, :LANES].astype(F32)
        ).astype(BF16)
        copies[2].start()
        for copy in copies:
            copy.wait()

    @pl.when(core == 0)
    def _():
        merge(keep_ref, got_ref)

    @pl.when(core == 1)
    def _():
        merge(got_ref, keep_ref)


def accumulators():
    kinds = []
    for m in range(2):
        kinds += [pltpu.ACC(m)((rows, 2 * LANES), F32) for rows in (64,) * DEPTH + (96, 96)]
    return kinds


def shaped(shape, dtype=F32):
    return jax.ShapeDtypeStruct(shape, dtype)


def local(spectra, supersat, cloud_flags, pair_kernel, rime_kernel, growth_matrix, fall_speed, density_factor):
    index = lax.axis_index("lat").astype(jnp.int32).reshape(1)
    swap = [(d, d ^ 1) for d in range(DEVS)]
    held = functools.partial(pltpu.with_memory_space_constraint, memory_space=pltpu.HBM)
    part = shaped((2, SENT, SLAB, MINE), BF16)
    tensor = shaped((BINS, BINS, BINS), BF16)
    sent, own, flag_rows, *parameters = pl.pallas_call(
        load_kernel,
        in_specs=[SMEM] + [HBM] * 8,
        out_specs=[VMEM] * 8,
        out_shape=[
            part,
            part,
            shaped((COLS // LANES, LANES), jnp.int32),
            tensor,
            tensor,
            shaped((BINS, 2, BINS), BF16),
            shaped((2, BINS)),
            shaped((1, LANES)),
        ],
        scratch_shapes=[pltpu.SemaphoreType.DMA((10,))],
        compiler_params=PARAMS,
        name="load_arguments",
    )(
        index, held(spectra), held(supersat), held(cloud_flags.reshape(COLS // LANES, LANES)), held(pair_kernel),
        held(rime_kernel), held(growth_matrix.transpose(1, 0, 2)), held(fall_speed), held(density_factor.reshape(1, LANES)),
    )
    other = lax.ppermute(sent, "lat", swap)

    state_shape = shaped((UNITS, SLAB, ROWS, LANES))
    flux_shape, flat_shape = shaped((FLAT, LANES), BF16), shaped((FLAT, LANES))
    level_shape = shaped((3 * SLAB, ROWS, LANES))
    cost = pl.CostEstimate(flops=2 * 2288 * 80 * SLAB * COLS, bytes_accessed=4_000_000, transcendentals=0)
    light = pl.CostEstimate(flops=1_000_000, bytes_accessed=8_000_000, transcendentals=0)

    main, rest, courant, inverse, lower = pl.pallas_call(
        table_kernel,
        in_specs=[SMEM] + [VMEM] * 5,
        out_specs=[VMEM] * 5,
        out_shape=[
            shaped((BINS, 64, LANES), BF16),
            shaped((2, 96, LANES), BF16),
            level_shape,
            level_shape,
            shaped((SLAB + 1, ROWS, LANES)),
        ],
        scratch_shapes=[
            pltpu.VMEM((HALF * (BINS - 1), LANES), F32),
            pltpu.VMEM((2 * BINS, LANES), F32),
        ],
        compiler_params=PARAMS,
        cost_estimate=light,
        name="tables",
    )(index, *parameters)

    state, flux, initial, sat, flags = pl.pallas_call(
        first_kernel,
        in_specs=[SMEM] + [VMEM] * 8,
        out_specs=[VMEM] * 5,
        out_shape=[
            state_shape,
            flux_shape,
            shaped((UNITS * SLAB * ROWS, LANES)),
            shaped((UNITS, 2 * SLAB, 1, LANES)),
            shaped((UNITS, 1, LANES)),
        ],
        compiler_params=PARAMS,
        cost_estimate=cost,
        name="first_substep",
    )(index, own, flag_rows, other, main, rest, courant, inverse, lower)

    arrive, weight = pl.pallas_call(
        weight_kernel,
        in_specs=[SMEM] + [VMEM] * 4 + [pl.BlockSpec(memory_space=pl.ANY)],
        out_specs=[VMEM] * 2,
        out_shape=[level_shape, shaped((7, FLAT, LANES))],
        scratch_shapes=[pltpu.VMEM((CHIPS, ROWS, LANES), F32)],
        compiler_params=PARAMS,
        cost_estimate=light,
        name="scan_weights",
    )(index, *parameters[3:], courant, inverse, flux)

    def between(pairs):
        return [(2 * a + c, 2 * b + c) for a, b in pairs for c in range(2)]

    around = []
    for r in range(1, GROUP):
        pairs = []
        for first in range(0, CHIPS, GROUP):
            size = min(GROUP, CHIPS - first)
            pairs += [(first + p, first + (p + r) % size) for p in range(size) if r < size]
        around.append(between([(a, b) for a, b in pairs if b not in (3, 6)]))
    near = between([(0, 3), (1, 4), (2, 5), (4, 6), (5, 7)])
    far = between([(0, 6), (1, 7)])

    def scan(flux):
        got = [lax.ppermute(flux, "lat", pairs) for pairs in around]
        prefix, send = pl.pallas_call(
            group_kernel,
            in_specs=[VMEM] * 4,
            out_specs=[VMEM] * 2,
            out_shape=[flat_shape, flux_shape],
            compiler_params=PARAMS,
            name="scan_group",
        )(flux, *got, weight)
        return prefix, lax.ppermute(send, "lat", far), lax.ppermute(send, "lat", near)

    state, flux = pl.pallas_call(
        second_kernel,
        in_specs=[VMEM] * 13,
        out_specs=[VMEM] * 2,
        out_shape=[state_shape, flux_shape],
        scratch_shapes=[pltpu.VMEM((UNITS, SLAB, ROWS, LANES), F32)],
        compiler_params=PARAMS,
        cost_estimate=cost,
        name="second_substep",
    )(state, *scan(flux), weight, sat, flags, main, rest, courant, inverse, arrive, lower)

    arrived = scan(flux)

    def tendencies(of_own, name):
        return pl.pallas_call(
            functools.partial(last_kernel, of_own),
            in_specs=[SMEM] + [VMEM] * 7,
            out_specs=VMEM,
            out_shape=shaped((2, BINS, SLAB, MINE), BF16),
            scratch_shapes=[pltpu.VMEM((3 * SLAB * ROWS, LANES), F32)],
            compiler_params=PARAMS,
            cost_estimate=light,
            name=name,
        )(index, state, initial, *arrived, weight, arrive)

    send = tendencies(False, "tendencies_sent")
    keep = tendencies(True, "tendencies_kept")

    got = lax.ppermute(send, "lat", swap)
    return pl.pallas_call(
        merge_kernel,
        in_specs=[SMEM] + [VMEM] * 2,
        out_specs=HBM,
        out_shape=shaped(spectra.shape, BF16),
        scratch_shapes=[pltpu.VMEM((2, BINS, SLAB, LANES), BF16), pltpu.SemaphoreType.DMA((3,))],
        compiler_params=PARAMS,
        cost_estimate=light,
        name="merge_slabs",
    )(index, keep, got)


def solution(mesh):
    return jax.shard_map(
        local,
        mesh=mesh,
        in_specs=(
            P(None, None, "lat", "lon"),
            P(None, "lat", "lon"),
            P("lon"),
            P(),
            P(),
            P(),
            P(),
            P(),
        ),
        out_specs=P(None, None, "lat", "lon"),
        check_vma=False,
    )
```

```python
import functools

import jax
import jax.numpy as jnp
from jax import lax
from jax.experimental import pallas as pl
from jax.experimental.pallas import tpu as pltpu
from jax.sharding import PartitionSpec as P

BINS = 33
HALF = 40
ROWS = 2 * HALF
SLAB = 8
COLS = 640
LANES = 128
MINE = 3 * LANES
SENT = BINS + 1
UNITS = 5
CHIPS = 8
GROUP = 3
DEVS = 2 * CHIPS
FLAT = 168
DEPTH = 11
F32 = jnp.float32
BF16 = jnp.bfloat16

VMEM = pl.BlockSpec(memory_space=pltpu.VMEM)
SMEM = pl.BlockSpec(memory_space=pltpu.SMEM)
HBM = pl.BlockSpec(memory_space=pltpu.HBM)
PARAMS = pltpu.CompilerParams(vmem_limit_bytes=24 * 1024 * 1024)


def on_left():
    return lax.broadcasted_iota(jnp.int32, (1, LANES), 1) < LANES // 2


def turned(value):
    return pltpu.roll(value, LANES // 2, 1)


def padded(value, rows, lanes):
    have_rows, have_lanes = value.shape
    if lanes > have_lanes:
        value = jnp.concatenate([value, jnp.zeros((have_rows, lanes - have_lanes), value.dtype)], axis=1)
    if rows > have_rows:
        value = jnp.concatenate([value, jnp.zeros((rows - have_rows, lanes), value.dtype)], axis=0)
    return value


def fall_column(fall_ref):
    row = lax.broadcasted_iota(jnp.int32, (HALF, BINS), 0)
    lane = lax.broadcasted_iota(jnp.int32, (HALF, BINS), 1)
    parts = []
    for s in range(2):
        spread = jnp.broadcast_to(fall_ref[s : s + 1, :], (HALF, BINS))
        parts.append(jnp.sum(jnp.where(row == lane, spread, 0.0), axis=1, keepdims=True))
    return jnp.concatenate(parts, axis=0)


def lane_of(value, lane):
    return jnp.broadcast_to(value[:, lane : lane + 1], (ROWS, LANES))


def settle_tables(courant, chip, courant_ref, inverse_ref, lower_ref):
    own = pltpu.roll(courant, lax.rem(LANES - 2 * SLAB * chip, LANES), 1)
    left = on_left()
    lower = None
    for l in range(2 * SLAB):
        here = lane_of(own, l)
        inverse = 1.0 / (1.0 + here)
        lower = None if l < SLAB else inverse if l == SLAB else lower * last * inverse
        last = here
        courant_ref[l] = here
        inverse_ref[l] = inverse
        if l >= SLAB:
            at = l - SLAB
            courant_ref[l + SLAB] = jnp.where(left, courant_ref[at], here)
            inverse_ref[l + SLAB] = jnp.where(left, inverse_ref[at], inverse)
            lower_ref[at] = jnp.where(left, 0.0, lower)
    lower_ref[SLAB] = jnp.where(left, 0.0, lower * last)


def arrive_table(courant_ref, inverse_ref, arrive_ref):
    left = on_left()
    arrive = inverse_ref[0]
    for l in range(2 * SLAB):
        if l > 0:
            arrive = arrive * courant_ref[l - 1] * inverse_ref[l]
        arrive_ref[l] = arrive
        if l >= SLAB:
            arrive_ref[l + SLAB] = jnp.where(left, arrive_ref[l - SLAB], arrive)


def flat_of(a, b, packed):
    middle = jnp.where(on_left(), turned(packed[HALF:]), packed[:HALF])
    pieces = (a[:HALF], a[HALF:], b[:HALF], b[HALF:], middle)
    row = lax.broadcasted_iota(jnp.int32, (8, LANES), 0)
    rest = jnp.zeros((8, LANES), F32)
    for at, piece in enumerate(pieces):
        tail = piece[32:]
        rest = jnp.where(row == at, tail if at == 0 else pltpu.roll(tail, at, 0), rest)
    return jnp.concatenate([piece[:32] for piece in pieces] + [rest], axis=0)


def from_flat(flat):
    row = lax.broadcasted_iota(jnp.int32, (8, LANES), 0)
    rest = flat[160:]
    pieces = []
    for at in range(5):
        tail = rest if at == 0 else pltpu.roll(rest, 8 - at, 0)
        pieces.append(jnp.concatenate([flat[32 * at : 32 * (at + 1)], jnp.where(row == 0, tail, 0.0)], axis=0))
    return pieces


def scan_weights(courant, chip, factor_ref, weight_ref):
    ratio = courant / (1.0 + courant)
    for step in (1, 2, 4, 8):
        ratio = ratio * pltpu.roll(ratio, LANES - step, 1)
    for e in range(CHIPS):
        factor_ref[e] = lane_of(ratio, 2 * SLAB * e)
    one = jnp.ones((ROWS, LANES), F32)

    def product(first, end):
        return lax.fori_loop(first, end, lambda e, w: w * factor_ref[e], one)

    place = chip % GROUP
    first = chip - place
    size = jnp.minimum(GROUP, CHIPS - first)
    for r in range(GROUP):
        there = jnp.where(place >= r, place - r, place - r + size)
        fits = there >= 0
        if r > 0:
            w = jnp.where(fits & (there < place), product(first + there + 1, chip), 0.0)
            weight_ref[r - 1] = flat_of(w, w, w)
        w = jnp.where(fits, product(first + there + 1, first + size), 0.0)
        weight_ref[2 + r] = flat_of(w, w, w)
    for at, start in ((5, first), (6, GROUP)):
        w = jnp.where(first >= GROUP, product(start, chip), 0.0)
        weight_ref[at] = flat_of(w, w, w)


def pack_weights(pair_ref, rime_ref, growth_ref, wide_ref, slim_ref, main_ref, rest_ref):
    for k in range(BINS):
        slim_ref[2 * k : 2 * k + 2, :] = padded(growth_ref[k].astype(F32), 2, LANES)
    for at, source in ((0, pair_ref), (1, rime_ref)):
        for k in range(BINS - 1):
            wide_ref[HALF * k : HALF * (k + 1), :] = padded(source[k].astype(F32), HALF, LANES)
        for i in range(BINS):
            main_ref[i, 32 * at : 32 * (at + 1), :] = wide_ref[pl.ds(i, 32, stride=HALF), :].astype(BF16)
        rest_ref[0, 48 * at : 48 * (at + 1), :] = padded(source[BINS - 1].astype(F32), 48, LANES).astype(BF16)
        grow = slim_ref[pl.ds(at, BINS, stride=2), :]
        rest_ref[1, 48 * at : 48 * (at + 1), :] = padded(grow, 48, LANES).astype(BF16)


def two_sided(block):
    half = block.shape[0] // 2
    empty = jnp.zeros((half, LANES), block.dtype)
    return jnp.concatenate(
        [
            jnp.concatenate([block[:half], empty], axis=1),
            jnp.concatenate([empty, block[half:]], axis=1),
        ],
        axis=0,
    )


def substep(round_ref, base_ref, state_ref, sat_ref, flag_ref, main_ref, rest_ref):
    steps = 2 * UNITS

    def place(step):
        block, first = step // 2, (step % 2) * 4
        return block, [(first + 2 * m, first + 2 * m + 1) for m in range(2)]

    def wide(ref, spot, rows, m):
        block, levels = spot
        return jnp.concatenate([ref[block, l, rows, :] for l in levels[m]], axis=1)

    def scoped(*accs):
        accs = (accs[: DEPTH + 2], accs[DEPTH + 2 :])

        def push(spot):
            empty = jnp.zeros((LANES - 48, 2 * LANES), BF16)
            for m in range(2):
                liquid = padded(wide(round_ref, spot, slice(0, HALF), m), 48, 2 * LANES).astype(BF16)
                frozen = padded(wide(round_ref, spot, slice(HALF, ROWS), m), 48, 2 * LANES).astype(BF16)
                pltpu.matmul_push_rhs(jnp.concatenate([liquid, empty, frozen, empty], axis=0), 0, m)

        def issue(j):
            lhs = two_sided(main_ref[j] if j < BINS else rest_ref[j - BINS])
            for m in range(2):
                acc = accs[m][j % DEPTH] if j < BINS else accs[m][DEPTH + j - BINS]
                pltpu.matmul_acc_lhs(acc, lhs, load_staged_rhs=0 if j == 0 else None)

        def body(step, carry):
            spot = place(step)
            block, levels = spot
            after = place(jnp.minimum(step + 1, steps - 1))
            sums = [jnp.zeros((64, 2 * LANES), F32) for m in range(2)]
            for i in range(BINS):
                if i == DEPTH - 1:
                    push(after)
                for m in range(2):
                    term = pltpu.matmul_pop(accs[m][i % DEPTH])
                    sums[m] = sums[m] + term * wide(round_ref, spot, slice(i, i + 1), m)
                if i + DEPTH < BINS:
                    issue(i + DEPTH)
                else:
                    if i + DEPTH == BINS:
                        issue(BINS)
                        issue(BINS + 1)
                    issue(i + DEPTH - BINS)
            flag = flag_ref[block]
            flag = jnp.concatenate([flag, flag], axis=1)
            for m in range(2):
                last = pltpu.matmul_pop(accs[m][DEPTH])
                grow = pltpu.matmul_pop(accs[m][DEPTH + 1])
                liquid = wide(round_ref, spot, slice(0, HALF), m)
                for s in range(2):
                    tail = jnp.sum(last[48 * s : 48 * s + HALF] * liquid, axis=0, keepdims=True)
                    tail = padded(tail, 8, 2 * LANES)
                    gain = jnp.concatenate([sums[m][32 * s : 32 * (s + 1)], tail], axis=0) * flag
                    sat = jnp.concatenate([sat_ref[block, s * SLAB + l] for l in levels[m]], axis=1)
                    gain = gain + grow[48 * s : 48 * s + HALF] * sat
                    for half, l in enumerate(levels[m]):
                        rows = slice(HALF * s, HALF * (s + 1))
                        part = gain[:, half * LANES : (half + 1) * LANES]
                        state_ref[block, l, rows, :] = base_ref[block, l, rows, :] + part
            return carry

        push(place(0))
        for j in range(DEPTH):
            issue(j)
        lax.fori_loop(0, steps, body, 0)
        for j in range(DEPTH):
            for m in range(2):
                pltpu.matmul_pop(accs[m][j])

    pl.run_scoped(scoped, *accumulators())


def settle(state_ref, courant_ref, inverse_ref, lower_ref, flux_ref):
    def column(units, first, levels):
        flux = None
        for at in range(levels):
            u, l = units[at // SLAB], at % SLAB
            state = state_ref[u, l] if flux is None else state_ref[u, l] + flux
            settled = state * inverse_ref[first + at]
            state_ref[u, l] = settled
            flux = courant_ref[first + at] * settled
        return flux

    a = column((0, 1), 0, 2 * SLAB)
    b = column((2, 3), 0, 2 * SLAB)
    packed = column((4,), 2 * SLAB, SLAB)
    upper = turned(packed)
    for l in range(SLAB):
        state_ref[4, l] = state_ref[4, l] + lower_ref[l] * upper
    packed = packed + lower_ref[SLAB] * upper
    flux_ref[...] = flat_of(a, b, packed).astype(BF16)


def arrivals(prefix_ref, far_refs, near_ref, weight_ref):
    far = sum(ref[...].astype(F32) for ref in far_refs)
    flux = prefix_ref[...] + weight_ref[5] * near_ref[...].astype(F32) + weight_ref[6] * far
    pieces = from_flat(flux)
    middle = pieces[4]
    other = turned(middle)
    left = on_left()
    packed = [jnp.where(left, other, middle), jnp.where(left, middle, other)]
    return tuple(jnp.concatenate(x, axis=0) for x in (pieces[0:2], pieces[2:4], packed))


def with_arrivals(state_ref, arrive_ref, fluxes, put):
    for u in range(UNITS):
        for l in range(SLAB):
            level = (l, SLAB + l, l, SLAB + l, 2 * SLAB + l)[u]
            put(u, l, state_ref[u, l] + arrive_ref[level] * fluxes[u // 2])


def table_kernel(
    index_ref, pair_ref, rime_ref, growth_ref, fall_ref, dens_ref,
    main_ref, rest_ref, courant_ref, inverse_ref, lower_ref,
    wide_ref, slim_ref,
):
    chip = index_ref[0] // 2
    courant = fall_column(fall_ref) * dens_ref[...]
    settle_tables(courant, chip, courant_ref, inverse_ref, lower_ref)
    pack_weights(pair_ref, rime_ref, growth_ref, wide_ref, slim_ref, main_ref, rest_ref)


def weight_kernel(index_ref, fall_ref, dens_ref, courant_ref, inverse_ref, flux_ref, arrive_ref, weight_ref, factor_ref):
    courant = fall_column(fall_ref) * dens_ref[...]
    arrive_table(courant_ref, inverse_ref, arrive_ref)
    scan_weights(courant, index_ref[0] // 2, factor_ref, weight_ref)


def load_kernel(
    index_ref, spectra_hbm, sat_hbm, flag_hbm, pair_hbm, rime_hbm, growth_hbm, fall_hbm, dens_hbm,
    sent_ref, own_ref, flag_ref, pair_ref, rime_ref, growth_ref, fall_ref, dens_ref,
    sems,
):
    core = index_ref[0] % 2
    pieces = []
    for at, ref in ((1 - core, sent_ref), (core, own_ref)):
        cols = pl.ds(pl.multiple_of(at * 2 * LANES, LANES), MINE)
        pieces.append((spectra_hbm.at[:, :, :, cols], ref.at[:, pl.ds(0, BINS)]))
        pieces.append((sat_hbm.at[:, :, cols], ref.at[:, BINS]))
    pieces += [(fall_hbm, fall_ref), (dens_hbm, dens_ref), (pair_hbm, pair_ref), (rime_hbm, rime_ref)]
    pieces += [(growth_hbm, growth_ref), (flag_hbm, flag_ref)]
    copies = [pltpu.make_async_copy(a, b, sems.at[n]) for n, (a, b) in enumerate(pieces)]
    for copy in copies:
        copy.start()
    for copy in copies:
        copy.wait()


def first_kernel(
    index_ref, own_ref, flag_row_ref, other_ref,
    main_ref, rest_ref, courant_ref, inverse_ref, lower_ref,
    state_ref, flux_ref, initial_ref, sat_ref, flag_ref,
):
    core = index_ref[0] % 2
    for u in range(UNITS):
        for l in range(SLAB):
            for s in range(2):
                row = u * SLAB * ROWS + ROWS * l + HALF * s + 32
                initial_ref[row : row + 8, :] = jnp.zeros((8, LANES), F32)
    a, b, middle = (pl.ds(pl.multiple_of(at * LANES, LANES), LANES) for at in (core, core + 1, 2 - 2 * core))
    first = core == 0
    own_half = on_left() == first

    def in_units(s, n):
        units = []
        for cols in (a, b):
            own, other = own_ref[s, n, :, cols].astype(F32), other_ref[s, n, :, cols].astype(F32)
            units += [jnp.where(first, own, other), jnp.where(first, other, own)]
        own, other = own_ref[s, n, :, middle].astype(F32), other_ref[s, n, :, middle].astype(F32)
        return units + [jnp.where(own_half, own, turned(other))]

    flags = (flag_row_ref[...] != 0).astype(F32)
    row_a, row_b = (jnp.where(first, flags[i : i + 1], flags[i + 3 : i + 4]) for i in range(2))
    flag_units = row_a, row_a, row_b, row_b, jnp.where(own_half, flags, turned(flags))[2:3]
    for u in range(UNITS):
        flag_ref[u] = flag_units[u]
    for s in range(2):
        units = in_units(s, BINS)
        for u in range(UNITS):
            for l in range(SLAB):
                sat_ref[u, s * SLAB + l] = units[u][l : l + 1]
        for n in range(BINS):
            units = in_units(s, n)
            for u in range(UNITS):
                initial_ref[pl.ds(u * SLAB * ROWS + HALF * s + n, SLAB, stride=ROWS), :] = units[u]
    initial = initial_ref.reshape(UNITS, SLAB, ROWS, LANES)
    substep(initial, initial, state_ref, sat_ref, flag_ref, main_ref, rest_ref)
    settle(state_ref, courant_ref, inverse_ref, lower_ref, flux_ref)


def second_kernel(
    state_in, prefix_ref, far_ref, near_ref, weight_ref, sat_ref, flag_ref, main_ref, rest_ref,
    courant_ref, inverse_ref, arrive_ref, lower_ref,
    state_ref, flux_ref,
    round_ref,
):
    def put(u, l, state):
        state_ref[u, l] = state
        round_ref[u, l] = state.astype(BF16).astype(F32)

    with_arrivals(state_in, arrive_ref, arrivals(prefix_ref, (far_ref,), near_ref, weight_ref), put)
    substep(round_ref, state_ref, state_ref, sat_ref, flag_ref, main_ref, rest_ref)
    settle(state_ref, courant_ref, inverse_ref, lower_ref, flux_ref)


def group_kernel(flux_ref, got1_ref, got2_ref, weight_ref, prefix_ref, send_ref):
    got1, got2 = got1_ref[...].astype(F32), got2_ref[...].astype(F32)
    prefix_ref[...] = weight_ref[0] * got1 + weight_ref[1] * got2
    total = weight_ref[2] * flux_ref[...].astype(F32) + weight_ref[3] * got1 + weight_ref[4] * got2
    send_ref[...] = total.astype(BF16)


def last_kernel(
    of_own, index_ref, state_ref, initial_ref, prefix_ref, farther_ref, far_ref, near_ref, weight_ref, arrive_ref,
    part_ref,
    change_ref,
):
    core = index_ref[0] % 2
    slab = core if of_own else 1 - core
    fluxes = arrivals(prefix_ref, (farther_ref, far_ref), near_ref, weight_ref)
    for k in range(3):
        u = 2 * k + slab if k < 2 else 4
        for l in range(SLAB):
            level = SLAB * slab + l if k < 2 else 2 * SLAB + l
            row = u * SLAB * ROWS + ROWS * l
            state = state_ref[u, l] + arrive_ref[level] * fluxes[k]
            start = initial_ref[pl.ds(pl.multiple_of(row, 8), ROWS), :]
            change_ref[(k * SLAB + l) * ROWS : (k * SLAB + l + 1) * ROWS, :] = (state - start) * 0.5
    spots = [pl.ds(pl.multiple_of(at * LANES, LANES), LANES) for at in (core, core + 1, 2 - 2 * core)]
    for s in range(2):
        for n in range(BINS):
            for k in range(3):
                rows = change_ref[pl.ds(k * SLAB * ROWS + HALF * s + n, SLAB, stride=ROWS), :]
                if k == 2 and not of_own:
                    rows = turned(rows)
                part_ref[s, n, :, spots[k]] = rows.astype(BF16)


def merge_kernel(index_ref, keep_ref, got_ref, out_hbm, middle_ref, sems):
    core = index_ref[0] % 2

    def merge(left_ref, right_ref):
        parts = [
            (left_ref.at[:, :, :, pl.ds(0, 2 * LANES)], out_hbm.at[:, :, :, pl.ds(0, 2 * LANES)]),
            (right_ref.at[:, :, :, pl.ds(LANES, 2 * LANES)], out_hbm.at[:, :, :, pl.ds(3 * LANES, 2 * LANES)]),
            (middle_ref, out_hbm.at[:, :, :, pl.ds(2 * LANES, LANES)]),
        ]
        copies = [pltpu.make_async_copy(x, y, sems.at[n]) for n, (x, y) in enumerate(parts)]
        copies[0].start()
        copies[1].start()
        side = lax.broadcasted_iota(jnp.int32, (2, BINS, SLAB, LANES), 3) < LANES // 2
        middle_ref[...] = jnp.where(
            side, left_ref[:, :, :, 2 * LANES :].astype(F32), right_ref[:, :, :, :LANES].astype(F32)
        ).astype(BF16)
        copies[2].start()
        for copy in copies:
            copy.wait()

    @pl.when(core == 0)
    def _():
        merge(keep_ref, got_ref)

    @pl.when(core == 1)
    def _():
        merge(got_ref, keep_ref)


def accumulators():
    kinds = []
    for m in range(2):
        kinds += [pltpu.ACC(m)((rows, 2 * LANES), F32) for rows in (64,) * DEPTH + (96, 96)]
    return kinds


def shaped(shape, dtype=F32):
    return jax.ShapeDtypeStruct(shape, dtype)


def local(spectra, supersat, cloud_flags, pair_kernel, rime_kernel, growth_matrix, fall_speed, density_factor):
    index = lax.axis_index("lat").astype(jnp.int32).reshape(1)
    swap = [(d, d ^ 1) for d in range(DEVS)]
    held = functools.partial(pltpu.with_memory_space_constraint, memory_space=pltpu.HBM)
    part = shaped((2, SENT, SLAB, MINE), BF16)
    tensor = shaped((BINS, BINS, BINS), BF16)
    sent, own, flag_rows, *parameters = pl.pallas_call(
        load_kernel,
        in_specs=[SMEM] + [HBM] * 8,
        out_specs=[VMEM] * 8,
        out_shape=[
            part,
            part,
            shaped((COLS // LANES, LANES), jnp.int32),
            tensor,
            tensor,
            shaped((BINS, 2, BINS), BF16),
            shaped((2, BINS)),
            shaped((1, LANES)),
        ],
        scratch_shapes=[pltpu.SemaphoreType.DMA((10,))],
        compiler_params=PARAMS,
        name="load_arguments",
    )(
        index, held(spectra), held(supersat), held(cloud_flags.reshape(COLS // LANES, LANES)), held(pair_kernel),
        held(rime_kernel), held(growth_matrix.transpose(1, 0, 2)), held(fall_speed), held(density_factor.reshape(1, LANES)),
    )
    other = lax.ppermute(sent, "lat", swap)

    state_shape = shaped((UNITS, SLAB, ROWS, LANES))
    flux_shape, flat_shape = shaped((FLAT, LANES), BF16), shaped((FLAT, LANES))
    level_shape = shaped((3 * SLAB, ROWS, LANES))
    cost = pl.CostEstimate(flops=2 * 2288 * 80 * SLAB * COLS, bytes_accessed=4_000_000, transcendentals=0)
    light = pl.CostEstimate(flops=1_000_000, bytes_accessed=8_000_000, transcendentals=0)

    main, rest, courant, inverse, lower = pl.pallas_call(
        table_kernel,
        in_specs=[SMEM] + [VMEM] * 5,
        out_specs=[VMEM] * 5,
        out_shape=[
            shaped((BINS, 64, LANES), BF16),
            shaped((2, 96, LANES), BF16),
            level_shape,
            level_shape,
            shaped((SLAB + 1, ROWS, LANES)),
        ],
        scratch_shapes=[
            pltpu.VMEM((HALF * (BINS - 1), LANES), F32),
            pltpu.VMEM((2 * BINS, LANES), F32),
        ],
        compiler_params=PARAMS,
        cost_estimate=light,
        name="tables",
    )(index, *parameters)

    state, flux, initial, sat, flags = pl.pallas_call(
        first_kernel,
        in_specs=[SMEM] + [VMEM] * 8,
        out_specs=[VMEM] * 5,
        out_shape=[
            state_shape,
            flux_shape,
            shaped((UNITS * SLAB * ROWS, LANES)),
            shaped((UNITS, 2 * SLAB, 1, LANES)),
            shaped((UNITS, 1, LANES)),
        ],
        compiler_params=PARAMS,
        cost_estimate=cost,
        name="first_substep",
    )(index, own, flag_rows, other, main, rest, courant, inverse, lower)

    arrive, weight = pl.pallas_call(
        weight_kernel,
        in_specs=[SMEM] + [VMEM] * 4 + [pl.BlockSpec(memory_space=pl.ANY)],
        out_specs=[VMEM] * 2,
        out_shape=[level_shape, shaped((7, FLAT, LANES))],
        scratch_shapes=[pltpu.VMEM((CHIPS, ROWS, LANES), F32)],
        compiler_params=PARAMS,
        cost_estimate=light,
        name="scan_weights",
    )(index, *parameters[3:], courant, inverse, flux)

    def between(pairs):
        return [(2 * a + c, 2 * b + c) for a, b in pairs for c in range(2)]

    def around(r, without):
        pairs = []
        for first in range(0, CHIPS, GROUP):
            size = min(GROUP, CHIPS - first)
            pairs += [(first + p, first + (p + r) % size) for p in range(size) if r < size]
        return between([(a, b) for a, b in pairs if b not in without])

    first_scan = (3, 6), ([(2, 4), (0, 6), (1, 7)], [(0, 3), (2, 5), (4, 6), (5, 7)])
    last_scan = (0, 3, 6), ([(1, 6)], [(2, 4), (1, 7)], [(1, 3), (2, 5), (4, 6), (5, 7)])

    def scan(flux, plan):
        without, sums = plan
        got = [lax.ppermute(flux, "lat", around(r, without)) for r in range(1, GROUP)]
        prefix, send = pl.pallas_call(
            group_kernel,
            in_specs=[VMEM] * 4,
            out_specs=[VMEM] * 2,
            out_shape=[flat_shape, flux_shape],
            compiler_params=PARAMS,
            name="scan_group",
        )(flux, *got, weight)
        return prefix, *(lax.ppermute(send, "lat", between(pairs)) for pairs in sums)

    state, flux = pl.pallas_call(
        second_kernel,
        in_specs=[VMEM] * 13,
        out_specs=[VMEM] * 2,
        out_shape=[state_shape, flux_shape],
        scratch_shapes=[pltpu.VMEM((UNITS, SLAB, ROWS, LANES), F32)],
        compiler_params=PARAMS,
        cost_estimate=cost,
        name="second_substep",
    )(state, *scan(flux, first_scan), weight, sat, flags, main, rest, courant, inverse, arrive, lower)

    arrived = scan(flux, last_scan)

    def tendencies(of_own, name):
        return pl.pallas_call(
            functools.partial(last_kernel, of_own),
            in_specs=[SMEM] + [VMEM] * 8,
            out_specs=VMEM,
            out_shape=shaped((2, BINS, SLAB, MINE), BF16),
            scratch_shapes=[pltpu.VMEM((3 * SLAB * ROWS, LANES), F32)],
            compiler_params=PARAMS,
            cost_estimate=light,
            name=name,
        )(index, state, initial, *arrived, weight, arrive)

    send = tendencies(False, "tendencies_sent")
    keep = tendencies(True, "tendencies_kept")

    got = lax.ppermute(send, "lat", swap)
    return pl.pallas_call(
        merge_kernel,
        in_specs=[SMEM] + [VMEM] * 2,
        out_specs=HBM,
        out_shape=shaped(spectra.shape, BF16),
        scratch_shapes=[pltpu.VMEM((2, BINS, SLAB, LANES), BF16), pltpu.SemaphoreType.DMA((3,))],
        compiler_params=PARAMS,
        cost_estimate=light,
        name="merge_slabs",
    )(index, keep, got)


def solution(mesh):
    return jax.shard_map(
        local,
        mesh=mesh,
        in_specs=(
            P(None, None, "lat", "lon"),
            P(None, "lat", "lon"),
            P("lon"),
            P(),
            P(),
            P(),
            P(),
            P(),
        ),
        out_specs=P(None, None, "lat", "lon"),
        check_vma=False,
    )
```

```python
import functools

import jax
import jax.numpy as jnp
from jax import lax
from jax.experimental import pallas as pl
from jax.experimental.pallas import tpu as pltpu
from jax.sharding import PartitionSpec as P

BINS = 33
HALF = 40
ROWS = 2 * HALF
SLAB = 8
COLS = 640
LANES = 128
MINE = 3 * LANES
SENT = BINS + 1
UNITS = 5
CHIPS = 8
GROUPS = ((0, 3), (3, 2), (5, 3))
FIRST_SCAN = (
    ([(0, 1), (1, 2), (2, 0), (3, 4), (4, 3), (5, 6), (6, 7)], [(0, 2), (1, 0), (2, 1), (5, 7)]),
    ([(1, 3), (2, 4), (3, 5), (0, 6), (4, 7)], [(0, 5), (4, 6), (1, 7)]),
)
LAST_SCAN = (
    ([(0, 1), (1, 2), (3, 4), (4, 3), (5, 6), (6, 7)], [(0, 2), (2, 1), (5, 7)]),
    ([(1, 3), (2, 4), (3, 5), (4, 6)], [(1, 7), (2, 5)], [(2, 6), (4, 7)]),
)
SUMS = FIRST_SCAN[1] + LAST_SCAN[1]
DEVS = 2 * CHIPS
FLAT = 168
DEPTH = 11
F32 = jnp.float32
BF16 = jnp.bfloat16

VMEM = pl.BlockSpec(memory_space=pltpu.VMEM)
SMEM = pl.BlockSpec(memory_space=pltpu.SMEM)
HBM = pl.BlockSpec(memory_space=pltpu.HBM)
PARAMS = pltpu.CompilerParams(vmem_limit_bytes=24 * 1024 * 1024)


def on_left():
    return lax.broadcasted_iota(jnp.int32, (1, LANES), 1) < LANES // 2


def turned(value):
    return pltpu.roll(value, LANES // 2, 1)


def padded(value, rows, lanes):
    have_rows, have_lanes = value.shape
    if lanes > have_lanes:
        value = jnp.concatenate([value, jnp.zeros((have_rows, lanes - have_lanes), value.dtype)], axis=1)
    if rows > have_rows:
        value = jnp.concatenate([value, jnp.zeros((rows - have_rows, lanes), value.dtype)], axis=0)
    return value


def fall_column(fall_ref):
    row = lax.broadcasted_iota(jnp.int32, (HALF, BINS), 0)
    lane = lax.broadcasted_iota(jnp.int32, (HALF, BINS), 1)
    parts = []
    for s in range(2):
        spread = jnp.broadcast_to(fall_ref[s : s + 1, :], (HALF, BINS))
        parts.append(jnp.sum(jnp.where(row == lane, spread, 0.0), axis=1, keepdims=True))
    return jnp.concatenate(parts, axis=0)


def lane_of(value, lane):
    return jnp.broadcast_to(value[:, lane : lane + 1], (ROWS, LANES))


def settle_tables(courant, chip, courant_ref, inverse_ref, lower_ref):
    own = pltpu.roll(courant, lax.rem(LANES - 2 * SLAB * chip, LANES), 1)
    left = on_left()
    lower = None
    for l in range(2 * SLAB):
        here = lane_of(own, l)
        inverse = 1.0 / (1.0 + here)
        lower = None if l < SLAB else inverse if l == SLAB else lower * last * inverse
        last = here
        courant_ref[l] = here
        inverse_ref[l] = inverse
        if l >= SLAB:
            at = l - SLAB
            courant_ref[l + SLAB] = jnp.where(left, courant_ref[at], here)
            inverse_ref[l + SLAB] = jnp.where(left, inverse_ref[at], inverse)
            lower_ref[at] = jnp.where(left, 0.0, lower)
    lower_ref[SLAB] = jnp.where(left, 0.0, lower * last)


def arrive_table(courant_ref, inverse_ref, arrive_ref):
    left = on_left()
    arrive = inverse_ref[0]
    for l in range(2 * SLAB):
        if l > 0:
            arrive = arrive * courant_ref[l - 1] * inverse_ref[l]
        arrive_ref[l] = arrive
        if l >= SLAB:
            arrive_ref[l + SLAB] = jnp.where(left, arrive_ref[l - SLAB], arrive)


def flat_of(a, b, packed):
    middle = jnp.where(on_left(), turned(packed[HALF:]), packed[:HALF])
    pieces = (a[:HALF], a[HALF:], b[:HALF], b[HALF:], middle)
    row = lax.broadcasted_iota(jnp.int32, (8, LANES), 0)
    rest = jnp.zeros((8, LANES), F32)
    for at, piece in enumerate(pieces):
        tail = piece[32:]
        rest = jnp.where(row == at, tail if at == 0 else pltpu.roll(tail, at, 0), rest)
    return jnp.concatenate([piece[:32] for piece in pieces] + [rest], axis=0)


def from_flat(flat):
    row = lax.broadcasted_iota(jnp.int32, (8, LANES), 0)
    rest = flat[160:]
    pieces = []
    for at in range(5):
        tail = rest if at == 0 else pltpu.roll(rest, 8 - at, 0)
        pieces.append(jnp.concatenate([flat[32 * at : 32 * (at + 1)], jnp.where(row == 0, tail, 0.0)], axis=0))
    return pieces


def scan_weights(courant, chip, factor_ref, weight_ref):
    ratio = courant / (1.0 + courant)
    for step in (1, 2, 4, 8):
        ratio = ratio * pltpu.roll(ratio, LANES - step, 1)
    for e in range(CHIPS):
        factor_ref[e] = lane_of(ratio, 2 * SLAB * e)
    one = jnp.ones((ROWS, LANES), F32)

    def product(first, end):
        return lax.fori_loop(first, end, lambda e, w: w * factor_ref[e], one)

    first, size = jnp.int32(GROUPS[0][0]), jnp.int32(GROUPS[0][1])
    for start, count in GROUPS[1:]:
        first, size = jnp.where(chip >= start, start, first), jnp.where(chip >= start, count, size)
    place = chip - first
    for r in range(3):
        there = jnp.where(place >= r, place - r, place - r + size)
        fits = there >= 0
        if r > 0:
            w = jnp.where(fits & (there < place), product(first + there + 1, chip), 0.0)
            weight_ref[r - 1] = flat_of(w, w, w)
        w = jnp.where(fits, product(first + there + 1, first + size), 0.0)
        weight_ref[2 + r] = flat_of(w, w, w)
    into = []
    for start, _ in GROUPS[1:]:
        w = jnp.where(chip >= start, product(start, chip), 0.0)
        into.append(flat_of(w, w, w))
    for n, pairs in enumerate(SUMS):
        of_first = functools.reduce(jnp.logical_or, [chip == b for a, b in pairs if a < GROUPS[1][0]], False)
        weight_ref[5 + n] = jnp.where(of_first, into[0], into[1])


def pack_weights(pair_ref, rime_ref, growth_ref, wide_ref, slim_ref, main_ref, rest_ref):
    for k in range(BINS):
        slim_ref[2 * k : 2 * k + 2, :] = padded(growth_ref[k].astype(F32), 2, LANES)
    for at, source in ((0, pair_ref), (1, rime_ref)):
        for k in range(BINS - 1):
            wide_ref[HALF * k : HALF * (k + 1), :] = padded(source[k].astype(F32), HALF, LANES)
        for i in range(BINS):
            main_ref[i, 32 * at : 32 * (at + 1), :] = wide_ref[pl.ds(i, 32, stride=HALF), :].astype(BF16)
        rest_ref[0, 48 * at : 48 * (at + 1), :] = padded(source[BINS - 1].astype(F32), 48, LANES).astype(BF16)
        grow = slim_ref[pl.ds(at, BINS, stride=2), :]
        rest_ref[1, 48 * at : 48 * (at + 1), :] = padded(grow, 48, LANES).astype(BF16)


def two_sided(block):
    half = block.shape[0] // 2
    empty = jnp.zeros((half, LANES), block.dtype)
    return jnp.concatenate(
        [
            jnp.concatenate([block[:half], empty], axis=1),
            jnp.concatenate([empty, block[half:]], axis=1),
        ],
        axis=0,
    )


def substep(round_ref, base_ref, state_ref, sat_ref, flag_ref, main_ref, rest_ref):
    steps = 2 * UNITS

    def place(step):
        block, first = step // 2, (step % 2) * 4
        return block, [(first + 2 * m, first + 2 * m + 1) for m in range(2)]

    def wide(ref, spot, rows, m):
        block, levels = spot
        return jnp.concatenate([ref[block, l, rows, :] for l in levels[m]], axis=1)

    def scoped(*accs):
        accs = (accs[: DEPTH + 2], accs[DEPTH + 2 :])

        def push(spot):
            empty = jnp.zeros((LANES - 48, 2 * LANES), BF16)
            for m in range(2):
                liquid = padded(wide(round_ref, spot, slice(0, HALF), m), 48, 2 * LANES).astype(BF16)
                frozen = padded(wide(round_ref, spot, slice(HALF, ROWS), m), 48, 2 * LANES).astype(BF16)
                pltpu.matmul_push_rhs(jnp.concatenate([liquid, empty, frozen, empty], axis=0), 0, m)

        def issue(j):
            lhs = two_sided(main_ref[j] if j < BINS else rest_ref[j - BINS])
            for m in range(2):
                acc = accs[m][j % DEPTH] if j < BINS else accs[m][DEPTH + j - BINS]
                pltpu.matmul_acc_lhs(acc, lhs, load_staged_rhs=0 if j == 0 else None)

        def body(step, carry):
            spot = place(step)
            block, levels = spot
            after = place(jnp.minimum(step + 1, steps - 1))
            sums = [jnp.zeros((64, 2 * LANES), F32) for m in range(2)]
            for i in range(BINS):
                if i == DEPTH - 1:
                    push(after)
                for m in range(2):
                    term = pltpu.matmul_pop(accs[m][i % DEPTH])
                    sums[m] = sums[m] + term * wide(round_ref, spot, slice(i, i + 1), m)
                if i + DEPTH < BINS:
                    issue(i + DEPTH)
                else:
                    if i + DEPTH == BINS:
                        issue(BINS)
                        issue(BINS + 1)
                    issue(i + DEPTH - BINS)
            flag = flag_ref[block]
            flag = jnp.concatenate([flag, flag], axis=1)
            for m in range(2):
                last = pltpu.matmul_pop(accs[m][DEPTH])
                grow = pltpu.matmul_pop(accs[m][DEPTH + 1])
                liquid = wide(round_ref, spot, slice(0, HALF), m)
                for s in range(2):
                    tail = jnp.sum(last[48 * s : 48 * s + HALF] * liquid, axis=0, keepdims=True)
                    tail = padded(tail, 8, 2 * LANES)
                    gain = jnp.concatenate([sums[m][32 * s : 32 * (s + 1)], tail], axis=0) * flag
                    sat = jnp.concatenate([sat_ref[block, s * SLAB + l] for l in levels[m]], axis=1)
                    gain = gain + grow[48 * s : 48 * s + HALF] * sat
                    for half, l in enumerate(levels[m]):
                        rows = slice(HALF * s, HALF * (s + 1))
                        part = gain[:, half * LANES : (half + 1) * LANES]
                        state_ref[block, l, rows, :] = base_ref[block, l, rows, :] + part
            return carry

        push(place(0))
        for j in range(DEPTH):
            issue(j)
        lax.fori_loop(0, steps, body, 0)
        for j in range(DEPTH):
            for m in range(2):
                pltpu.matmul_pop(accs[m][j])

    pl.run_scoped(scoped, *accumulators())


def settle(state_ref, courant_ref, inverse_ref, lower_ref, flux_ref):
    def column(units, first, levels):
        flux = None
        for at in range(levels):
            u, l = units[at // SLAB], at % SLAB
            state = state_ref[u, l] if flux is None else state_ref[u, l] + flux
            settled = state * inverse_ref[first + at]
            state_ref[u, l] = settled
            flux = courant_ref[first + at] * settled
        return flux

    a = column((0, 1), 0, 2 * SLAB)
    b = column((2, 3), 0, 2 * SLAB)
    packed = column((4,), 2 * SLAB, SLAB)
    upper = turned(packed)
    for l in range(SLAB):
        state_ref[4, l] = state_ref[4, l] + lower_ref[l] * upper
    packed = packed + lower_ref[SLAB] * upper
    flux_ref[...] = flat_of(a, b, packed).astype(BF16)


def arrivals(prefix_ref, got_refs, weight_ref, at):
    flux = prefix_ref[...]
    for n, ref in enumerate(reversed(got_refs)):
        flux = flux + weight_ref[at + n] * ref[...].astype(F32)
    pieces = from_flat(flux)
    middle = pieces[4]
    other = turned(middle)
    left = on_left()
    packed = [jnp.where(left, other, middle), jnp.where(left, middle, other)]
    return tuple(jnp.concatenate(x, axis=0) for x in (pieces[0:2], pieces[2:4], packed))


def with_arrivals(state_ref, arrive_ref, fluxes, put):
    for u in range(UNITS):
        for l in range(SLAB):
            level = (l, SLAB + l, l, SLAB + l, 2 * SLAB + l)[u]
            put(u, l, state_ref[u, l] + arrive_ref[level] * fluxes[u // 2])


def table_kernel(
    index_ref, pair_ref, rime_ref, growth_ref, fall_ref, dens_ref,
    main_ref, rest_ref, courant_ref, inverse_ref, lower_ref,
    wide_ref, slim_ref,
):
    chip = index_ref[0] // 2
    courant = fall_column(fall_ref) * dens_ref[...]
    settle_tables(courant, chip, courant_ref, inverse_ref, lower_ref)
    pack_weights(pair_ref, rime_ref, growth_ref, wide_ref, slim_ref, main_ref, rest_ref)


def weight_kernel(index_ref, fall_ref, dens_ref, courant_ref, inverse_ref, flux_ref, arrive_ref, weight_ref, factor_ref):
    courant = fall_column(fall_ref) * dens_ref[...]
    arrive_table(courant_ref, inverse_ref, arrive_ref)
    scan_weights(courant, index_ref[0] // 2, factor_ref, weight_ref)


def load_kernel(
    index_ref, spectra_hbm, sat_hbm, flag_hbm, pair_hbm, rime_hbm, growth_hbm, fall_hbm, dens_hbm,
    sent_ref, own_ref, flag_ref, pair_ref, rime_ref, growth_ref, fall_ref, dens_ref,
    sems,
):
    core = index_ref[0] % 2
    pieces = []
    for at, ref in ((1 - core, sent_ref), (core, own_ref)):
        cols = pl.ds(pl.multiple_of(at * 2 * LANES, LANES), MINE)
        pieces.append((spectra_hbm.at[:, :, :, cols], ref.at[:, pl.ds(0, BINS)]))
        pieces.append((sat_hbm.at[:, :, cols], ref.at[:, BINS]))
    pieces += [(fall_hbm, fall_ref), (dens_hbm, dens_ref), (pair_hbm, pair_ref), (rime_hbm, rime_ref)]
    pieces += [(growth_hbm, growth_ref), (flag_hbm, flag_ref)]
    copies = [pltpu.make_async_copy(a, b, sems.at[n]) for n, (a, b) in enumerate(pieces)]
    for copy in copies:
        copy.start()
    for copy in copies:
        copy.wait()


def first_kernel(
    index_ref, own_ref, flag_row_ref, other_ref,
    main_ref, rest_ref, courant_ref, inverse_ref, lower_ref,
    state_ref, flux_ref, initial_ref, sat_ref, flag_ref,
):
    core = index_ref[0] % 2
    for u in range(UNITS):
        for l in range(SLAB):
            for s in range(2):
                row = u * SLAB * ROWS + ROWS * l + HALF * s + 32
                initial_ref[row : row + 8, :] = jnp.zeros((8, LANES), F32)
    a, b, middle = (pl.ds(pl.multiple_of(at * LANES, LANES), LANES) for at in (core, core + 1, 2 - 2 * core))
    first = core == 0
    own_half = on_left() == first

    def in_units(s, n):
        units = []
        for cols in (a, b):
            own, other = own_ref[s, n, :, cols].astype(F32), other_ref[s, n, :, cols].astype(F32)
            units += [jnp.where(first, own, other), jnp.where(first, other, own)]
        own, other = own_ref[s, n, :, middle].astype(F32), other_ref[s, n, :, middle].astype(F32)
        return units + [jnp.where(own_half, own, turned(other))]

    flags = (flag_row_ref[...] != 0).astype(F32)
    row_a, row_b = (jnp.where(first, flags[i : i + 1], flags[i + 3 : i + 4]) for i in range(2))
    flag_units = row_a, row_a, row_b, row_b, jnp.where(own_half, flags, turned(flags))[2:3]
    for u in range(UNITS):
        flag_ref[u] = flag_units[u]
    for s in range(2):
        units = in_units(s, BINS)
        for u in range(UNITS):
            for l in range(SLAB):
                sat_ref[u, s * SLAB + l] = units[u][l : l + 1]
        for n in range(BINS):
            units = in_units(s, n)
            for u in range(UNITS):
                initial_ref[pl.ds(u * SLAB * ROWS + HALF * s + n, SLAB, stride=ROWS), :] = units[u]
    initial = initial_ref.reshape(UNITS, SLAB, ROWS, LANES)
    substep(initial, initial, state_ref, sat_ref, flag_ref, main_ref, rest_ref)
    settle(state_ref, courant_ref, inverse_ref, lower_ref, flux_ref)


def second_kernel(
    state_in, prefix_ref, far_ref, near_ref, weight_ref, sat_ref, flag_ref, main_ref, rest_ref,
    courant_ref, inverse_ref, arrive_ref, lower_ref,
    state_ref, flux_ref,
    round_ref,
):
    def put(u, l, state):
        state_ref[u, l] = state
        round_ref[u, l] = state.astype(BF16).astype(F32)

    with_arrivals(state_in, arrive_ref, arrivals(prefix_ref, (far_ref, near_ref), weight_ref, 5), put)
    substep(round_ref, state_ref, state_ref, sat_ref, flag_ref, main_ref, rest_ref)
    settle(state_ref, courant_ref, inverse_ref, lower_ref, flux_ref)


def group_kernel(flux_ref, got1_ref, got2_ref, weight_ref, prefix_ref, send_ref):
    got1, got2 = got1_ref[...].astype(F32), got2_ref[...].astype(F32)
    prefix_ref[...] = weight_ref[0] * got1 + weight_ref[1] * got2
    total = weight_ref[2] * flux_ref[...].astype(F32) + weight_ref[3] * got1 + weight_ref[4] * got2
    send_ref[...] = total.astype(BF16)


def last_kernel(
    of_own, index_ref, state_ref, initial_ref, prefix_ref, farther_ref, far_ref, near_ref, weight_ref, arrive_ref,
    part_ref,
    change_ref,
):
    core = index_ref[0] % 2
    slab = core if of_own else 1 - core
    fluxes = arrivals(prefix_ref, (farther_ref, far_ref, near_ref), weight_ref, 5 + len(FIRST_SCAN[1]))
    for k in range(3):
        u = 2 * k + slab if k < 2 else 4
        for l in range(SLAB):
            level = SLAB * slab + l if k < 2 else 2 * SLAB + l
            row = u * SLAB * ROWS + ROWS * l
            state = state_ref[u, l] + arrive_ref[level] * fluxes[k]
            start = initial_ref[pl.ds(pl.multiple_of(row, 8), ROWS), :]
            change_ref[(k * SLAB + l) * ROWS : (k * SLAB + l + 1) * ROWS, :] = (state - start) * 0.5
    spots = [pl.ds(pl.multiple_of(at * LANES, LANES), LANES) for at in (core, core + 1, 2 - 2 * core)]
    for s in range(2):
        for n in range(BINS):
            for k in range(3):
                rows = change_ref[pl.ds(k * SLAB * ROWS + HALF * s + n, SLAB, stride=ROWS), :]
                if k == 2 and not of_own:
                    rows = turned(rows)
                part_ref[s, n, :, spots[k]] = rows.astype(BF16)


def merge_kernel(index_ref, keep_ref, got_ref, out_hbm, middle_ref, sems):
    core = index_ref[0] % 2

    def merge(left_ref, right_ref):
        parts = [
            (left_ref.at[:, :, :, pl.ds(0, 2 * LANES)], out_hbm.at[:, :, :, pl.ds(0, 2 * LANES)]),
            (right_ref.at[:, :, :, pl.ds(LANES, 2 * LANES)], out_hbm.at[:, :, :, pl.ds(3 * LANES, 2 * LANES)]),
            (middle_ref, out_hbm.at[:, :, :, pl.ds(2 * LANES, LANES)]),
        ]
        copies = [pltpu.make_async_copy(x, y, sems.at[n]) for n, (x, y) in enumerate(parts)]
        copies[0].start()
        copies[1].start()
        side = lax.broadcasted_iota(jnp.int32, (2, BINS, SLAB, LANES), 3) < LANES // 2
        middle_ref[...] = jnp.where(
            side, left_ref[:, :, :, 2 * LANES :].astype(F32), right_ref[:, :, :, :LANES].astype(F32)
        ).astype(BF16)
        copies[2].start()
        for copy in copies:
            copy.wait()

    @pl.when(core == 0)
    def _():
        merge(keep_ref, got_ref)

    @pl.when(core == 1)
    def _():
        merge(got_ref, keep_ref)


def accumulators():
    kinds = []
    for m in range(2):
        kinds += [pltpu.ACC(m)((rows, 2 * LANES), F32) for rows in (64,) * DEPTH + (96, 96)]
    return kinds


def shaped(shape, dtype=F32):
    return jax.ShapeDtypeStruct(shape, dtype)


def local(spectra, supersat, cloud_flags, pair_kernel, rime_kernel, growth_matrix, fall_speed, density_factor):
    index = lax.axis_index("lat").astype(jnp.int32).reshape(1)
    swap = [(d, d ^ 1) for d in range(DEVS)]
    held = functools.partial(pltpu.with_memory_space_constraint, memory_space=pltpu.HBM)
    part = shaped((2, SENT, SLAB, MINE), BF16)
    tensor = shaped((BINS, BINS, BINS), BF16)
    sent, own, flag_rows, *parameters = pl.pallas_call(
        load_kernel,
        in_specs=[SMEM] + [HBM] * 8,
        out_specs=[VMEM] * 8,
        out_shape=[
            part,
            part,
            shaped((COLS // LANES, LANES), jnp.int32),
            tensor,
            tensor,
            shaped((BINS, 2, BINS), BF16),
            shaped((2, BINS)),
            shaped((1, LANES)),
        ],
        scratch_shapes=[pltpu.SemaphoreType.DMA((10,))],
        compiler_params=PARAMS,
        name="load_arguments",
    )(
        index, held(spectra), held(supersat), held(cloud_flags.reshape(COLS // LANES, LANES)), held(pair_kernel),
        held(rime_kernel), held(growth_matrix.transpose(1, 0, 2)), held(fall_speed), held(density_factor.reshape(1, LANES)),
    )
    other = lax.ppermute(sent, "lat", swap)

    state_shape = shaped((UNITS, SLAB, ROWS, LANES))
    flux_shape, flat_shape = shaped((FLAT, LANES), BF16), shaped((FLAT, LANES))
    level_shape = shaped((3 * SLAB, ROWS, LANES))
    cost = pl.CostEstimate(flops=2 * 2288 * 80 * SLAB * COLS, bytes_accessed=4_000_000, transcendentals=0)
    light = pl.CostEstimate(flops=1_000_000, bytes_accessed=8_000_000, transcendentals=0)

    main, rest, courant, inverse, lower = pl.pallas_call(
        table_kernel,
        in_specs=[SMEM] + [VMEM] * 5,
        out_specs=[VMEM] * 5,
        out_shape=[
            shaped((BINS, 64, LANES), BF16),
            shaped((2, 96, LANES), BF16),
            level_shape,
            level_shape,
            shaped((SLAB + 1, ROWS, LANES)),
        ],
        scratch_shapes=[
            pltpu.VMEM((HALF * (BINS - 1), LANES), F32),
            pltpu.VMEM((2 * BINS, LANES), F32),
        ],
        compiler_params=PARAMS,
        cost_estimate=light,
        name="tables",
    )(index, *parameters)

    state, flux, initial, sat, flags = pl.pallas_call(
        first_kernel,
        in_specs=[SMEM] + [VMEM] * 8,
        out_specs=[VMEM] * 5,
        out_shape=[
            state_shape,
            flux_shape,
            shaped((UNITS * SLAB * ROWS, LANES)),
            shaped((UNITS, 2 * SLAB, 1, LANES)),
            shaped((UNITS, 1, LANES)),
        ],
        compiler_params=PARAMS,
        cost_estimate=cost,
        name="first_substep",
    )(index, own, flag_rows, other, main, rest, courant, inverse, lower)

    arrive, weight = pl.pallas_call(
        weight_kernel,
        in_specs=[SMEM] + [VMEM] * 4 + [pl.BlockSpec(memory_space=pl.ANY)],
        out_specs=[VMEM] * 2,
        out_shape=[level_shape, shaped((5 + len(SUMS), FLAT, LANES))],
        scratch_shapes=[pltpu.VMEM((CHIPS, ROWS, LANES), F32)],
        compiler_params=PARAMS,
        cost_estimate=light,
        name="scan_weights",
    )(index, *parameters[3:], courant, inverse, flux)

    def between(pairs):
        return [(2 * a + c, 2 * b + c) for a, b in pairs for c in range(2)]

    def scan(flux, plan):
        own, sums = plan
        got = [lax.ppermute(flux, "lat", between(pairs)) for pairs in own]
        prefix, send = pl.pallas_call(
            group_kernel,
            in_specs=[VMEM] * 4,
            out_specs=[VMEM] * 2,
            out_shape=[flat_shape, flux_shape],
            compiler_params=PARAMS,
            name="scan_group",
        )(flux, *got, weight)
        return prefix, *(lax.ppermute(send, "lat", between(pairs)) for pairs in reversed(sums))

    state, flux = pl.pallas_call(
        second_kernel,
        in_specs=[VMEM] * 13,
        out_specs=[VMEM] * 2,
        out_shape=[state_shape, flux_shape],
        scratch_shapes=[pltpu.VMEM((UNITS, SLAB, ROWS, LANES), F32)],
        compiler_params=PARAMS,
        cost_estimate=cost,
        name="second_substep",
    )(state, *scan(flux, FIRST_SCAN), weight, sat, flags, main, rest, courant, inverse, arrive, lower)

    arrived = scan(flux, LAST_SCAN)

    def tendencies(of_own, name):
        return pl.pallas_call(
            functools.partial(last_kernel, of_own),
            in_specs=[SMEM] + [VMEM] * 8,
            out_specs=VMEM,
            out_shape=shaped((2, BINS, SLAB, MINE), BF16),
            scratch_shapes=[pltpu.VMEM((3 * SLAB * ROWS, LANES), F32)],
            compiler_params=PARAMS,
            cost_estimate=light,
            name=name,
        )(index, state, initial, *arrived, weight, arrive)

    send = tendencies(False, "tendencies_sent")
    keep = tendencies(True, "tendencies_kept")

    got = lax.ppermute(send, "lat", swap)
    return pl.pallas_call(
        merge_kernel,
        in_specs=[SMEM] + [VMEM] * 2,
        out_specs=HBM,
        out_shape=shaped(spectra.shape, BF16),
        scratch_shapes=[pltpu.VMEM((2, BINS, SLAB, LANES), BF16), pltpu.SemaphoreType.DMA((3,))],
        compiler_params=PARAMS,
        cost_estimate=light,
        name="merge_slabs",
    )(index, keep, got)


def solution(mesh):
    return jax.shard_map(
        local,
        mesh=mesh,
        in_specs=(
            P(None, None, "lat", "lon"),
            P(None, "lat", "lon"),
            P("lon"),
            P(),
            P(),
            P(),
            P(),
            P(),
        ),
        out_specs=P(None, None, "lat", "lon"),
        check_vma=False,
    )
```

```python
import functools

import jax
import jax.numpy as jnp
from jax import lax
from jax.experimental import pallas as pl
from jax.experimental.pallas import tpu as pltpu
from jax.sharding import PartitionSpec as P

BINS = 33
HALF = 40
ROWS = 2 * HALF
SLAB = 8
COLS = 640
LANES = 128
MINE = 3 * LANES
SENT = BINS + 1
UNITS = 5
CHIPS = 8
GROUPS = ((0, 3), (3, 2), (5, 3))
FIRST_SCAN = (
    ([(0, 1), (1, 2), (2, 0), (3, 4), (4, 3), (5, 6), (6, 7)], [(0, 2), (1, 0), (2, 1), (5, 7)]),
    ([(1, 3), (2, 4), (3, 5), (0, 6), (4, 7)], [(0, 5), (4, 6), (1, 7)]),
)
LAST_SCAN = (
    ([(0, 1), (1, 2), (3, 4), (4, 3), (5, 6), (6, 7)], [(0, 2), (2, 1), (5, 7)]),
    ([(1, 3), (2, 4), (3, 5), (4, 6)], [(1, 7), (2, 5)], [(2, 6), (4, 7)]),
)
SUMS = FIRST_SCAN[1] + LAST_SCAN[1]
DEVS = 2 * CHIPS
FLAT = 168
DEPTH = 10
SQUARE = tuple(range(24, 32))
SINGLES = tuple(i for i in range(BINS) if i not in SQUARE)
PAIRS = tuple(zip(SQUARE[::2], SQUARE[1::2]))
BLOCKS = len(SINGLES) + len(PAIRS) + 1
PRODUCTS = 48
F32 = jnp.float32
BF16 = jnp.bfloat16

VMEM = pl.BlockSpec(memory_space=pltpu.VMEM)
SMEM = pl.BlockSpec(memory_space=pltpu.SMEM)
HBM = pl.BlockSpec(memory_space=pltpu.HBM)
PARAMS = pltpu.CompilerParams(vmem_limit_bytes=24 * 1024 * 1024)


def on_left():
    return lax.broadcasted_iota(jnp.int32, (1, LANES), 1) < LANES // 2


def turned(value):
    return pltpu.roll(value, LANES // 2, 1)


def padded(value, rows, lanes):
    have_rows, have_lanes = value.shape
    if lanes > have_lanes:
        value = jnp.concatenate([value, jnp.zeros((have_rows, lanes - have_lanes), value.dtype)], axis=1)
    if rows > have_rows:
        value = jnp.concatenate([value, jnp.zeros((rows - have_rows, lanes), value.dtype)], axis=0)
    return value


def fall_column(fall_ref):
    row = lax.broadcasted_iota(jnp.int32, (HALF, BINS), 0)
    lane = lax.broadcasted_iota(jnp.int32, (HALF, BINS), 1)
    parts = []
    for s in range(2):
        spread = jnp.broadcast_to(fall_ref[s : s + 1, :], (HALF, BINS))
        parts.append(jnp.sum(jnp.where(row == lane, spread, 0.0), axis=1, keepdims=True))
    return jnp.concatenate(parts, axis=0)


def lane_of(value, lane):
    return jnp.broadcast_to(value[:, lane : lane + 1], (ROWS, LANES))


def settle_tables(courant, chip, courant_ref, inverse_ref, lower_ref):
    own = pltpu.roll(courant, lax.rem(LANES - 2 * SLAB * chip, LANES), 1)
    left = on_left()
    lower = None
    for l in range(2 * SLAB):
        here = lane_of(own, l)
        inverse = 1.0 / (1.0 + here)
        lower = None if l < SLAB else inverse if l == SLAB else lower * last * inverse
        last = here
        courant_ref[l] = here
        inverse_ref[l] = inverse
        if l >= SLAB:
            at = l - SLAB
            courant_ref[l + SLAB] = jnp.where(left, courant_ref[at], here)
            inverse_ref[l + SLAB] = jnp.where(left, inverse_ref[at], inverse)
            lower_ref[at] = jnp.where(left, 0.0, lower)
    lower_ref[SLAB] = jnp.where(left, 0.0, lower * last)


def arrive_table(courant_ref, inverse_ref, arrive_ref):
    left = on_left()
    arrive = inverse_ref[0]
    for l in range(2 * SLAB):
        if l > 0:
            arrive = arrive * courant_ref[l - 1] * inverse_ref[l]
        arrive_ref[l] = arrive
        if l >= SLAB:
            arrive_ref[l + SLAB] = jnp.where(left, arrive_ref[l - SLAB], arrive)


def flat_of(a, b, packed):
    middle = jnp.where(on_left(), turned(packed[HALF:]), packed[:HALF])
    pieces = (a[:HALF], a[HALF:], b[:HALF], b[HALF:], middle)
    row = lax.broadcasted_iota(jnp.int32, (8, LANES), 0)
    rest = jnp.zeros((8, LANES), F32)
    for at, piece in enumerate(pieces):
        tail = piece[32:]
        rest = jnp.where(row == at, tail if at == 0 else pltpu.roll(tail, at, 0), rest)
    return jnp.concatenate([piece[:32] for piece in pieces] + [rest], axis=0)


def from_flat(flat):
    row = lax.broadcasted_iota(jnp.int32, (8, LANES), 0)
    rest = flat[160:]
    pieces = []
    for at in range(5):
        tail = rest if at == 0 else pltpu.roll(rest, 8 - at, 0)
        pieces.append(jnp.concatenate([flat[32 * at : 32 * (at + 1)], jnp.where(row == 0, tail, 0.0)], axis=0))
    return pieces


def scan_weights(courant, chip, factor_ref, weight_ref):
    ratio = courant / (1.0 + courant)
    for step in (1, 2, 4, 8):
        ratio = ratio * pltpu.roll(ratio, LANES - step, 1)
    for e in range(CHIPS):
        factor_ref[e] = lane_of(ratio, 2 * SLAB * e)
    one = jnp.ones((ROWS, LANES), F32)

    def product(first, end):
        return lax.fori_loop(first, end, lambda e, w: w * factor_ref[e], one)

    first, size = jnp.int32(GROUPS[0][0]), jnp.int32(GROUPS[0][1])
    for start, count in GROUPS[1:]:
        first, size = jnp.where(chip >= start, start, first), jnp.where(chip >= start, count, size)
    place = chip - first
    for r in range(3):
        there = jnp.where(place >= r, place - r, place - r + size)
        fits = there >= 0
        if r > 0:
            w = jnp.where(fits & (there < place), product(first + there + 1, chip), 0.0)
            weight_ref[r - 1] = flat_of(w, w, w)
        w = jnp.where(fits, product(first + there + 1, first + size), 0.0)
        weight_ref[2 + r] = flat_of(w, w, w)
    into = []
    for start, _ in GROUPS[1:]:
        w = jnp.where(chip >= start, product(start, chip), 0.0)
        into.append(flat_of(w, w, w))
    for n, pairs in enumerate(SUMS):
        of_first = functools.reduce(jnp.logical_or, [chip == b for a, b in pairs if a < GROUPS[1][0]], False)
        weight_ref[5 + n] = jnp.where(of_first, into[0], into[1])


def pack_weights(pair_ref, rime_ref, growth_ref, wide_ref, slim_ref, main_ref, rest_ref):
    for k in range(BINS):
        slim_ref[2 * k : 2 * k + 2, :] = padded(growth_ref[k].astype(F32), 2, LANES)
    low, size = SQUARE[0], len(SQUARE)
    lane = lax.broadcasted_iota(jnp.int32, (1, LANES), 1)
    in_square = (lane >= low) & (lane < low + size)
    for at, source in ((0, pair_ref), (1, rime_ref)):
        for k in range(BINS - 1):
            wide_ref[HALF * k : HALF * (k + 1), :] = padded(source[k].astype(F32), HALF, LANES)
        if at == 0:
            products = jnp.zeros((32, LANES), F32)
            for i in range(size):
                rows = wide_ref[pl.ds(low + i, 32, stride=HALF), :]
                products = products + pltpu.roll(jnp.where(in_square, rows, 0.0), PRODUCTS + size * i - low, 1)
            main_ref[BLOCKS - 1, :32, :] = products.astype(BF16)
            main_ref[BLOCKS - 1, 32:, :] = jnp.zeros((32, LANES), BF16)
            for first in range(0, BINS - 1, LANES // size):
                ks = range(first, min(first + LANES // size, BINS - 1))
                turn = jnp.concatenate([wide_ref[HALF * k + low : HALF * k + low + size, :] for k in ks], axis=0).T
                for n, k in enumerate(ks):
                    shift = (low - size * n) % LANES
                    extra = pltpu.roll(turn[:HALF], shift, 1) if shift else turn[:HALF]
                    rows = slice(HALF * k, HALF * (k + 1))
                    wide_ref[rows, :] = wide_ref[rows, :] + jnp.where(in_square, extra, 0.0)
            for j, i in enumerate(SINGLES):
                main_ref[j, :32, :] = wide_ref[pl.ds(i, 32, stride=HALF), :].astype(BF16)
        else:
            places = [(j, 32, i) for j, i in enumerate(SINGLES)]
            places += [(len(SINGLES) + n, 32 * half, i) for n, pair in enumerate(PAIRS) for half, i in enumerate(pair)]
            for j, row, i in places:
                main_ref[j, row : row + 32, :] = wide_ref[pl.ds(i, 32, stride=HALF), :].astype(BF16)
        rest_ref[0, 48 * at : 48 * (at + 1), :] = padded(source[BINS - 1].astype(F32), 48, LANES).astype(BF16)
        grow = slim_ref[pl.ds(at, BINS, stride=2), :]
        rest_ref[1, 48 * at : 48 * (at + 1), :] = padded(grow, 48, LANES).astype(BF16)


def two_sided(block):
    half = block.shape[0] // 2
    empty = jnp.zeros((half, LANES), block.dtype)
    return jnp.concatenate(
        [
            jnp.concatenate([block[:half], empty], axis=1),
            jnp.concatenate([empty, block[half:]], axis=1),
        ],
        axis=0,
    )


def substep(round_ref, base_ref, state_ref, sat_ref, flag_ref, main_ref, rest_ref):
    steps = 2 * UNITS

    def place(step):
        block, first = step // 2, (step % 2) * 4
        return block, [(first + 2 * m, first + 2 * m + 1) for m in range(2)]

    def wide(ref, spot, rows, m):
        block, levels = spot
        return jnp.concatenate([ref[block, l, rows, :] for l in levels[m]], axis=1)

    def scoped(*accs):
        accs = (accs[: DEPTH + 3], accs[DEPTH + 3 :])

        def push(spot):
            empty = jnp.zeros((LANES - 48, 2 * LANES), BF16)
            for m in range(2):
                liquid = padded(wide(round_ref, spot, slice(0, HALF), m), 48, 2 * LANES).astype(BF16)
                square = wide(round_ref, spot, slice(SQUARE[0], SQUARE[-1] + 1), m)
                products = [square * wide(round_ref, spot, slice(i, i + 1), m) for i in SQUARE]
                products = padded(jnp.concatenate(products, axis=0), LANES - PRODUCTS, 2 * LANES).astype(BF16)
                frozen = padded(wide(round_ref, spot, slice(HALF, ROWS), m), 48, 2 * LANES).astype(BF16)
                pltpu.matmul_push_rhs(jnp.concatenate([liquid, products, frozen, empty], axis=0), 0, m)

        def issue(j):
            if j >= BLOCKS:
                lhs = two_sided(rest_ref[j - BLOCKS])
            elif j < len(SINGLES):
                lhs = two_sided(main_ref[j])
            elif j < BLOCKS - 1:
                lhs = jnp.concatenate([jnp.zeros((64, LANES), BF16), main_ref[j]], axis=1)
            else:
                lhs = jnp.concatenate([main_ref[j, :32, :], jnp.zeros((32, LANES), BF16)], axis=1)
            for m in range(2):
                pltpu.matmul_acc_lhs(place_of(m, j), lhs, load_staged_rhs=0 if j == 0 else None)

        def place_of(m, j):
            return accs[m][j % DEPTH if j < BLOCKS - 1 else DEPTH + j - (BLOCKS - 1)]

        def body(step, carry):
            spot = place(step)
            block, levels = spot
            after = place(jnp.minimum(step + 1, steps - 1))
            sums = [[jnp.zeros((32, 2 * LANES), F32) for s in range(2)] for m in range(2)]
            for i in range(BLOCKS):
                if i == DEPTH - 1:
                    push(after)
                for m in range(2):
                    term = pltpu.matmul_pop(place_of(m, i))
                    if i < len(SINGLES):
                        by = wide(round_ref, spot, slice(SINGLES[i], SINGLES[i] + 1), m)
                        sums[m] = [sums[m][s] + term[32 * s : 32 * (s + 1)] * by for s in range(2)]
                    elif i < BLOCKS - 1:
                        for half, at in enumerate(PAIRS[i - len(SINGLES)]):
                            by = wide(round_ref, spot, slice(at, at + 1), m)
                            sums[m][1] = sums[m][1] + term[32 * half : 32 * (half + 1)] * by
                    else:
                        sums[m][0] = sums[m][0] + term
                if i + DEPTH < BLOCKS:
                    issue(i + DEPTH)
                else:
                    if i + DEPTH == BLOCKS:
                        issue(BLOCKS)
                        issue(BLOCKS + 1)
                    issue(i + DEPTH - BLOCKS)
            flag = flag_ref[block]
            flag = jnp.concatenate([flag, flag], axis=1)
            for m in range(2):
                last = pltpu.matmul_pop(place_of(m, BLOCKS))
                grow = pltpu.matmul_pop(place_of(m, BLOCKS + 1))
                liquid = wide(round_ref, spot, slice(0, HALF), m)
                for s in range(2):
                    tail = jnp.sum(last[48 * s : 48 * s + HALF] * liquid, axis=0, keepdims=True)
                    tail = padded(tail, 8, 2 * LANES)
                    gain = jnp.concatenate([sums[m][s], tail], axis=0) * flag
                    sat = jnp.concatenate([sat_ref[block, s * SLAB + l] for l in levels[m]], axis=1)
                    gain = gain + grow[48 * s : 48 * s + HALF] * sat
                    for half, l in enumerate(levels[m]):
                        rows = slice(HALF * s, HALF * (s + 1))
                        part = gain[:, half * LANES : (half + 1) * LANES]
                        state_ref[block, l, rows, :] = base_ref[block, l, rows, :] + part
            return carry

        push(place(0))
        for j in range(DEPTH):
            issue(j)
        lax.fori_loop(0, steps, body, 0)
        for j in range(DEPTH):
            for m in range(2):
                pltpu.matmul_pop(accs[m][j])

    pl.run_scoped(scoped, *accumulators())


def settle(state_ref, courant_ref, inverse_ref, lower_ref, flux_ref):
    def column(units, first, levels):
        flux = None
        for at in range(levels):
            u, l = units[at // SLAB], at % SLAB
            state = state_ref[u, l] if flux is None else state_ref[u, l] + flux
            settled = state * inverse_ref[first + at]
            state_ref[u, l] = settled
            flux = courant_ref[first + at] * settled
        return flux

    a = column((0, 1), 0, 2 * SLAB)
    b = column((2, 3), 0, 2 * SLAB)
    packed = column((4,), 2 * SLAB, SLAB)
    upper = turned(packed)
    for l in range(SLAB):
        state_ref[4, l] = state_ref[4, l] + lower_ref[l] * upper
    packed = packed + lower_ref[SLAB] * upper
    flux_ref[...] = flat_of(a, b, packed).astype(BF16)


def arrivals(prefix_ref, got_refs, weight_ref, at):
    flux = prefix_ref[...]
    for n, ref in enumerate(reversed(got_refs)):
        flux = flux + weight_ref[at + n] * ref[...].astype(F32)
    pieces = from_flat(flux)
    middle = pieces[4]
    other = turned(middle)
    left = on_left()
    packed = [jnp.where(left, other, middle), jnp.where(left, middle, other)]
    return tuple(jnp.concatenate(x, axis=0) for x in (pieces[0:2], pieces[2:4], packed))


def with_arrivals(state_ref, arrive_ref, fluxes, put):
    for u in range(UNITS):
        for l in range(SLAB):
            level = (l, SLAB + l, l, SLAB + l, 2 * SLAB + l)[u]
            put(u, l, state_ref[u, l] + arrive_ref[level] * fluxes[u // 2])


def table_kernel(
    index_ref, pair_ref, rime_ref, growth_ref, fall_ref, dens_ref,
    main_ref, rest_ref, courant_ref, inverse_ref, lower_ref,
    wide_ref, slim_ref,
):
    chip = index_ref[0] // 2
    courant = fall_column(fall_ref) * dens_ref[...]
    settle_tables(courant, chip, courant_ref, inverse_ref, lower_ref)
    pack_weights(pair_ref, rime_ref, growth_ref, wide_ref, slim_ref, main_ref, rest_ref)


def weight_kernel(index_ref, fall_ref, dens_ref, courant_ref, inverse_ref, flux_ref, arrive_ref, weight_ref, factor_ref):
    courant = fall_column(fall_ref) * dens_ref[...]
    arrive_table(courant_ref, inverse_ref, arrive_ref)
    scan_weights(courant, index_ref[0] // 2, factor_ref, weight_ref)


def load_kernel(
    index_ref, spectra_hbm, sat_hbm, flag_hbm, pair_hbm, rime_hbm, growth_hbm, fall_hbm, dens_hbm,
    sent_ref, own_ref, flag_ref, pair_ref, rime_ref, growth_ref, fall_ref, dens_ref,
    sems,
):
    core = index_ref[0] % 2
    pieces = []
    for at, ref in ((1 - core, sent_ref), (core, own_ref)):
        cols = pl.ds(pl.multiple_of(at * 2 * LANES, LANES), MINE)
        pieces.append((spectra_hbm.at[:, :, :, cols], ref.at[:, pl.ds(0, BINS)]))
        pieces.append((sat_hbm.at[:, :, cols], ref.at[:, BINS]))
    pieces += [(fall_hbm, fall_ref), (dens_hbm, dens_ref), (pair_hbm, pair_ref), (rime_hbm, rime_ref)]
    pieces += [(growth_hbm, growth_ref), (flag_hbm, flag_ref)]
    copies = [pltpu.make_async_copy(a, b, sems.at[n]) for n, (a, b) in enumerate(pieces)]
    for copy in copies:
        copy.start()
    for copy in copies:
        copy.wait()


def first_kernel(
    index_ref, own_ref, flag_row_ref, other_ref,
    main_ref, rest_ref, courant_ref, inverse_ref, lower_ref,
    state_ref, flux_ref, initial_ref, sat_ref, flag_ref,
):
    core = index_ref[0] % 2
    for u in range(UNITS):
        for l in range(SLAB):
            for s in range(2):
                row = u * SLAB * ROWS + ROWS * l + HALF * s + 32
                initial_ref[row : row + 8, :] = jnp.zeros((8, LANES), F32)
    a, b, middle = (pl.ds(pl.multiple_of(at * LANES, LANES), LANES) for at in (core, core + 1, 2 - 2 * core))
    first = core == 0
    own_half = on_left() == first

    def in_units(s, n):
        units = []
        for cols in (a, b):
            own, other = own_ref[s, n, :, cols].astype(F32), other_ref[s, n, :, cols].astype(F32)
            units += [jnp.where(first, own, other), jnp.where(first, other, own)]
        own, other = own_ref[s, n, :, middle].astype(F32), other_ref[s, n, :, middle].astype(F32)
        return units + [jnp.where(own_half, own, turned(other))]

    flags = (flag_row_ref[...] != 0).astype(F32)
    row_a, row_b = (jnp.where(first, flags[i : i + 1], flags[i + 3 : i + 4]) for i in range(2))
    flag_units = row_a, row_a, row_b, row_b, jnp.where(own_half, flags, turned(flags))[2:3]
    for u in range(UNITS):
        flag_ref[u] = flag_units[u]
    for s in range(2):
        units = in_units(s, BINS)
        for u in range(UNITS):
            for l in range(SLAB):
                sat_ref[u, s * SLAB + l] = units[u][l : l + 1]
        for n in range(BINS):
            units = in_units(s, n)
            for u in range(UNITS):
                initial_ref[pl.ds(u * SLAB * ROWS + HALF * s + n, SLAB, stride=ROWS), :] = units[u]
    initial = initial_ref.reshape(UNITS, SLAB, ROWS, LANES)
    substep(initial, initial, state_ref, sat_ref, flag_ref, main_ref, rest_ref)
    settle(state_ref, courant_ref, inverse_ref, lower_ref, flux_ref)


def second_kernel(
    state_in, prefix_ref, far_ref, near_ref, weight_ref, sat_ref, flag_ref, main_ref, rest_ref,
    courant_ref, inverse_ref, arrive_ref, lower_ref,
    state_ref, flux_ref,
    round_ref,
):
    def put(u, l, state):
        state_ref[u, l] = state
        round_ref[u, l] = state.astype(BF16).astype(F32)

    with_arrivals(state_in, arrive_ref, arrivals(prefix_ref, (far_ref, near_ref), weight_ref, 5), put)
    substep(round_ref, state_ref, state_ref, sat_ref, flag_ref, main_ref, rest_ref)
    settle(state_ref, courant_ref, inverse_ref, lower_ref, flux_ref)


def group_kernel(flux_ref, got1_ref, got2_ref, weight_ref, prefix_ref, send_ref):
    got1, got2 = got1_ref[...].astype(F32), got2_ref[...].astype(F32)
    prefix_ref[...] = weight_ref[0] * got1 + weight_ref[1] * got2
    total = weight_ref[2] * flux_ref[...].astype(F32) + weight_ref[3] * got1 + weight_ref[4] * got2
    send_ref[...] = total.astype(BF16)


def last_kernel(
    of_own, index_ref, state_ref, initial_ref, prefix_ref, farther_ref, far_ref, near_ref, weight_ref, arrive_ref,
    part_ref,
    change_ref,
):
    core = index_ref[0] % 2
    slab = core if of_own else 1 - core
    fluxes = arrivals(prefix_ref, (farther_ref, far_ref, near_ref), weight_ref, 5 + len(FIRST_SCAN[1]))
    for k in range(3):
        u = 2 * k + slab if k < 2 else 4
        for l in range(SLAB):
            level = SLAB * slab + l if k < 2 else 2 * SLAB + l
            row = u * SLAB * ROWS + ROWS * l
            state = state_ref[u, l] + arrive_ref[level] * fluxes[k]
            start = initial_ref[pl.ds(pl.multiple_of(row, 8), ROWS), :]
            change_ref[(k * SLAB + l) * ROWS : (k * SLAB + l + 1) * ROWS, :] = (state - start) * 0.5
    spots = [pl.ds(pl.multiple_of(at * LANES, LANES), LANES) for at in (core, core + 1, 2 - 2 * core)]
    for s in range(2):
        for n in range(BINS):
            for k in range(3):
                rows = change_ref[pl.ds(k * SLAB * ROWS + HALF * s + n, SLAB, stride=ROWS), :]
                if k == 2 and not of_own:
                    rows = turned(rows)
                part_ref[s, n, :, spots[k]] = rows.astype(BF16)


def merge_kernel(index_ref, keep_ref, got_ref, out_hbm, middle_ref, sems):
    core = index_ref[0] % 2

    def merge(left_ref, right_ref):
        parts = [
            (left_ref.at[:, :, :, pl.ds(0, 2 * LANES)], out_hbm.at[:, :, :, pl.ds(0, 2 * LANES)]),
            (right_ref.at[:, :, :, pl.ds(LANES, 2 * LANES)], out_hbm.at[:, :, :, pl.ds(3 * LANES, 2 * LANES)]),
            (middle_ref, out_hbm.at[:, :, :, pl.ds(2 * LANES, LANES)]),
        ]
        copies = [pltpu.make_async_copy(x, y, sems.at[n]) for n, (x, y) in enumerate(parts)]
        copies[0].start()
        copies[1].start()
        side = lax.broadcasted_iota(jnp.int32, (2, BINS, SLAB, LANES), 3) < LANES // 2
        middle_ref[...] = jnp.where(
            side, left_ref[:, :, :, 2 * LANES :].astype(F32), right_ref[:, :, :, :LANES].astype(F32)
        ).astype(BF16)
        copies[2].start()
        for copy in copies:
            copy.wait()

    @pl.when(core == 0)
    def _():
        merge(keep_ref, got_ref)

    @pl.when(core == 1)
    def _():
        merge(got_ref, keep_ref)


def accumulators():
    kinds = []
    for m in range(2):
        kinds += [pltpu.ACC(m)((rows, 2 * LANES), F32) for rows in (64,) * DEPTH + (32, 96, 96)]
    return kinds


def shaped(shape, dtype=F32):
    return jax.ShapeDtypeStruct(shape, dtype)


def local(spectra, supersat, cloud_flags, pair_kernel, rime_kernel, growth_matrix, fall_speed, density_factor):
    index = lax.axis_index("lat").astype(jnp.int32).reshape(1)
    swap = [(d, d ^ 1) for d in range(DEVS)]
    held = functools.partial(pltpu.with_memory_space_constraint, memory_space=pltpu.HBM)
    part = shaped((2, SENT, SLAB, MINE), BF16)
    tensor = shaped((BINS, BINS, BINS), BF16)
    sent, own, flag_rows, *parameters = pl.pallas_call(
        load_kernel,
        in_specs=[SMEM] + [HBM] * 8,
        out_specs=[VMEM] * 8,
        out_shape=[
            part,
            part,
            shaped((COLS // LANES, LANES), jnp.int32),
            tensor,
            tensor,
            shaped((BINS, 2, BINS), BF16),
            shaped((2, BINS)),
            shaped((1, LANES)),
        ],
        scratch_shapes=[pltpu.SemaphoreType.DMA((10,))],
        compiler_params=PARAMS,
        name="load_arguments",
    )(
        index, held(spectra), held(supersat), held(cloud_flags.reshape(COLS // LANES, LANES)), held(pair_kernel),
        held(rime_kernel), held(growth_matrix.transpose(1, 0, 2)), held(fall_speed), held(density_factor.reshape(1, LANES)),
    )
    other = lax.ppermute(sent, "lat", swap)

    state_shape = shaped((UNITS, SLAB, ROWS, LANES))
    flux_shape, flat_shape = shaped((FLAT, LANES), BF16), shaped((FLAT, LANES))
    level_shape = shaped((3 * SLAB, ROWS, LANES))
    cost = pl.CostEstimate(flops=2 * 2288 * 80 * SLAB * COLS, bytes_accessed=4_000_000, transcendentals=0)
    light = pl.CostEstimate(flops=1_000_000, bytes_accessed=8_000_000, transcendentals=0)

    main, rest, courant, inverse, lower = pl.pallas_call(
        table_kernel,
        in_specs=[SMEM] + [VMEM] * 5,
        out_specs=[VMEM] * 5,
        out_shape=[
            shaped((BLOCKS, 64, LANES), BF16),
            shaped((2, 96, LANES), BF16),
            level_shape,
            level_shape,
            shaped((SLAB + 1, ROWS, LANES)),
        ],
        scratch_shapes=[
            pltpu.VMEM((HALF * (BINS - 1), LANES), F32),
            pltpu.VMEM((2 * BINS, LANES), F32),
        ],
        compiler_params=PARAMS,
        cost_estimate=light,
        name="tables",
    )(index, *parameters)

    state, flux, initial, sat, flags = pl.pallas_call(
        first_kernel,
        in_specs=[SMEM] + [VMEM] * 8,
        out_specs=[VMEM] * 5,
        out_shape=[
            state_shape,
            flux_shape,
            shaped((UNITS * SLAB * ROWS, LANES)),
            shaped((UNITS, 2 * SLAB, 1, LANES)),
            shaped((UNITS, 1, LANES)),
        ],
        compiler_params=PARAMS,
        cost_estimate=cost,
        name="first_substep",
    )(index, own, flag_rows, other, main, rest, courant, inverse, lower)

    arrive, weight = pl.pallas_call(
        weight_kernel,
        in_specs=[SMEM] + [VMEM] * 4 + [pl.BlockSpec(memory_space=pl.ANY)],
        out_specs=[VMEM] * 2,
        out_shape=[level_shape, shaped((5 + len(SUMS), FLAT, LANES))],
        scratch_shapes=[pltpu.VMEM((CHIPS, ROWS, LANES), F32)],
        compiler_params=PARAMS,
        cost_estimate=light,
        name="scan_weights",
    )(index, *parameters[3:], courant, inverse, flux)

    def between(pairs):
        return [(2 * a + c, 2 * b + c) for a, b in pairs for c in range(2)]

    def scan(flux, plan):
        own, sums = plan
        got = [lax.ppermute(flux, "lat", between(pairs)) for pairs in own]
        prefix, send = pl.pallas_call(
            group_kernel,
            in_specs=[VMEM] * 4,
            out_specs=[VMEM] * 2,
            out_shape=[flat_shape, flux_shape],
            compiler_params=PARAMS,
            name="scan_group",
        )(flux, *got, weight)
        return prefix, *(lax.ppermute(send, "lat", between(pairs)) for pairs in reversed(sums))

    state, flux = pl.pallas_call(
        second_kernel,
        in_specs=[VMEM] * 13,
        out_specs=[VMEM] * 2,
        out_shape=[state_shape, flux_shape],
        scratch_shapes=[pltpu.VMEM((UNITS, SLAB, ROWS, LANES), F32)],
        compiler_params=PARAMS,
        cost_estimate=cost,
        name="second_substep",
    )(state, *scan(flux, FIRST_SCAN), weight, sat, flags, main, rest, courant, inverse, arrive, lower)

    arrived = scan(flux, LAST_SCAN)

    def tendencies(of_own, name):
        return pl.pallas_call(
            functools.partial(last_kernel, of_own),
            in_specs=[SMEM] + [VMEM] * 8,
            out_specs=VMEM,
            out_shape=shaped((2, BINS, SLAB, MINE), BF16),
            scratch_shapes=[pltpu.VMEM((3 * SLAB * ROWS, LANES), F32)],
            compiler_params=PARAMS,
            cost_estimate=light,
            name=name,
        )(index, state, initial, *arrived, weight, arrive)

    send = tendencies(False, "tendencies_sent")
    keep = tendencies(True, "tendencies_kept")

    got = lax.ppermute(send, "lat", swap)
    return pl.pallas_call(
        merge_kernel,
        in_specs=[SMEM] + [VMEM] * 2,
        out_specs=HBM,
        out_shape=shaped(spectra.shape, BF16),
        scratch_shapes=[pltpu.VMEM((2, BINS, SLAB, LANES), BF16), pltpu.SemaphoreType.DMA((3,))],
        compiler_params=PARAMS,
        cost_estimate=light,
        name="merge_slabs",
    )(index, keep, got)


def solution(mesh):
    return jax.shard_map(
        local,
        mesh=mesh,
        in_specs=(
            P(None, None, "lat", "lon"),
            P(None, "lat", "lon"),
            P("lon"),
            P(),
            P(),
            P(),
            P(),
            P(),
        ),
        out_specs=P(None, None, "lat", "lon"),
        check_vma=False,
    )
```

```python
import functools

import jax
import jax.numpy as jnp
from jax import lax
from jax.experimental import pallas as pl
from jax.experimental.pallas import tpu as pltpu
from jax.sharding import PartitionSpec as P

BINS = 33
HALF = 40
ROWS = 2 * HALF
SLAB = 8
COLS = 640
LANES = 128
MINE = 3 * LANES
SENT = BINS + 1
UNITS = 5
CHIPS = 8
GROUPS = ((0, 3), (3, 2), (5, 3))
FIRST_SCAN = (
    ([(0, 1), (1, 2), (2, 0), (3, 4), (4, 3), (5, 6), (6, 7)], [(0, 2), (1, 0), (2, 1), (5, 7)]),
    ([(1, 3), (2, 4), (3, 5), (0, 6), (4, 7)], [(0, 5), (4, 6), (1, 7)]),
)
LAST_SCAN = (
    ([(0, 1), (1, 2), (3, 4), (4, 3), (5, 6), (6, 7)], [(0, 2), (2, 1), (5, 7)]),
    ([(1, 3), (2, 4), (3, 5), (4, 6)], [(1, 7), (2, 5)], [(2, 6), (4, 7)]),
)
SUMS = FIRST_SCAN[1] + LAST_SCAN[1]
DEVS = 2 * CHIPS
FLAT = 168
DEPTH = 13
SQUARE = tuple(range(16, 32))
SINGLES = tuple(i for i in range(BINS) if i not in SQUARE)
PAIRS = tuple(zip(SQUARE[::2], SQUARE[1::2]))
BLOCKS = len(SINGLES) + len(PAIRS) + 1
PRODUCTS = 48
TURNS = (0, 1, 2, 3, 4), (5, 6, 7, 8)
F32 = jnp.float32
BF16 = jnp.bfloat16

VMEM = pl.BlockSpec(memory_space=pltpu.VMEM)
SMEM = pl.BlockSpec(memory_space=pltpu.SMEM)
HBM = pl.BlockSpec(memory_space=pltpu.HBM)
PARAMS = pltpu.CompilerParams(vmem_limit_bytes=24 * 1024 * 1024)


def on_left():
    return lax.broadcasted_iota(jnp.int32, (1, LANES), 1) < LANES // 2


def turned(value):
    return pltpu.roll(value, LANES // 2, 1)


def padded(value, rows, lanes):
    have_rows, have_lanes = value.shape
    if lanes > have_lanes:
        value = jnp.concatenate([value, jnp.zeros((have_rows, lanes - have_lanes), value.dtype)], axis=1)
    if rows > have_rows:
        value = jnp.concatenate([value, jnp.zeros((rows - have_rows, lanes), value.dtype)], axis=0)
    return value


def fall_column(fall_ref):
    row = lax.broadcasted_iota(jnp.int32, (HALF, BINS), 0)
    lane = lax.broadcasted_iota(jnp.int32, (HALF, BINS), 1)
    parts = []
    for s in range(2):
        spread = jnp.broadcast_to(fall_ref[s : s + 1, :], (HALF, BINS))
        parts.append(jnp.sum(jnp.where(row == lane, spread, 0.0), axis=1, keepdims=True))
    return jnp.concatenate(parts, axis=0)


def lane_of(value, lane):
    return jnp.broadcast_to(value[:, lane : lane + 1], (ROWS, LANES))


def settle_tables(courant, chip, courant_ref, inverse_ref, lower_ref):
    own = pltpu.roll(courant, lax.rem(LANES - 2 * SLAB * chip, LANES), 1)
    left = on_left()
    lower = None
    for l in range(2 * SLAB):
        here = lane_of(own, l)
        inverse = 1.0 / (1.0 + here)
        lower = None if l < SLAB else inverse if l == SLAB else lower * last * inverse
        last = here
        courant_ref[l] = here
        inverse_ref[l] = inverse
        if l >= SLAB:
            at = l - SLAB
            courant_ref[l + SLAB] = jnp.where(left, courant_ref[at], here)
            inverse_ref[l + SLAB] = jnp.where(left, inverse_ref[at], inverse)
            lower_ref[at] = jnp.where(left, 0.0, lower)
    lower_ref[SLAB] = jnp.where(left, 0.0, lower * last)


def arrive_table(courant_ref, inverse_ref, arrive_ref):
    left = on_left()
    arrive = inverse_ref[0]
    for l in range(2 * SLAB):
        if l > 0:
            arrive = arrive * courant_ref[l - 1] * inverse_ref[l]
        arrive_ref[l] = arrive
        if l >= SLAB:
            arrive_ref[l + SLAB] = jnp.where(left, arrive_ref[l - SLAB], arrive)


def flat_of(a, b, packed):
    middle = jnp.where(on_left(), turned(packed[HALF:]), packed[:HALF])
    pieces = (a[:HALF], a[HALF:], b[:HALF], b[HALF:], middle)
    row = lax.broadcasted_iota(jnp.int32, (8, LANES), 0)
    rest = jnp.zeros((8, LANES), F32)
    for at, piece in enumerate(pieces):
        tail = piece[32:]
        rest = jnp.where(row == at, tail if at == 0 else pltpu.roll(tail, at, 0), rest)
    return jnp.concatenate([piece[:32] for piece in pieces] + [rest], axis=0)


def from_flat(flat):
    row = lax.broadcasted_iota(jnp.int32, (8, LANES), 0)
    rest = flat[160:]
    pieces = []
    for at in range(5):
        tail = rest if at == 0 else pltpu.roll(rest, 8 - at, 0)
        pieces.append(jnp.concatenate([flat[32 * at : 32 * (at + 1)], jnp.where(row == 0, tail, 0.0)], axis=0))
    return pieces


def scan_weights(courant, chip, factor_ref, weight_ref):
    ratio = courant / (1.0 + courant)
    for step in (1, 2, 4, 8):
        ratio = ratio * pltpu.roll(ratio, LANES - step, 1)
    for e in range(CHIPS):
        factor_ref[e] = lane_of(ratio, 2 * SLAB * e)
    one = jnp.ones((ROWS, LANES), F32)

    def product(first, end):
        return lax.fori_loop(first, end, lambda e, w: w * factor_ref[e], one)

    first, size = jnp.int32(GROUPS[0][0]), jnp.int32(GROUPS[0][1])
    for start, count in GROUPS[1:]:
        first, size = jnp.where(chip >= start, start, first), jnp.where(chip >= start, count, size)
    place = chip - first
    for r in range(3):
        there = jnp.where(place >= r, place - r, place - r + size)
        fits = there >= 0
        if r > 0:
            w = jnp.where(fits & (there < place), product(first + there + 1, chip), 0.0)
            weight_ref[r - 1] = flat_of(w, w, w)
        w = jnp.where(fits, product(first + there + 1, first + size), 0.0)
        weight_ref[2 + r] = flat_of(w, w, w)
    into = []
    for start, _ in GROUPS[1:]:
        w = jnp.where(chip >= start, product(start, chip), 0.0)
        into.append(flat_of(w, w, w))
    for n, pairs in enumerate(SUMS):
        of_first = functools.reduce(jnp.logical_or, [chip == b for a, b in pairs if a < GROUPS[1][0]], False)
        weight_ref[5 + n] = jnp.where(of_first, into[0], into[1])


def pack_weights(pair_ref, rime_ref, growth_ref, wide_ref, slim_ref, main_ref, rest_ref):
    for k in range(BINS):
        slim_ref[2 * k : 2 * k + 2, :] = padded(growth_ref[k].astype(F32), 2, LANES)
    low, size = SQUARE[0], len(SQUARE)
    lane = lax.broadcasted_iota(jnp.int32, (1, LANES), 1)
    in_square = (lane >= low) & (lane < low + size)
    for at, source in ((0, pair_ref), (1, rime_ref)):
        for k in range(BINS - 1):
            wide_ref[HALF * k : HALF * (k + 1), :] = padded(source[k].astype(F32), HALF, LANES)
        if at == 0:
            for first in range(0, BINS - 1, LANES // size):
                ks = range(first, min(first + LANES // size, BINS - 1))
                turn = jnp.concatenate([wide_ref[HALF * k + low : HALF * k + low + size, :] for k in ks], axis=0).T
                for n, k in enumerate(ks):
                    shift = (low - size * n) % LANES
                    extra = pltpu.roll(turn[:HALF], shift, 1) if shift else turn[:HALF]
                    rows = slice(HALF * k, HALF * (k + 1))
                    wide_ref[rows, :] = wide_ref[rows, :] + jnp.where(in_square, extra, 0.0)
            for half, turns in enumerate(TURNS):
                products = jnp.zeros((32, LANES), F32)
                for i in range(size):
                    rows = wide_ref[pl.ds(low + i, 32, stride=HALF), :]
                    for n, r in enumerate(turns):
                        if 2 * r < size or i < size // 2:
                            to, there = PRODUCTS + size * n + i, low + (i + r) % size
                            moved = pltpu.roll(rows, (to - there) % LANES, 1) if to != there else rows
                            products = jnp.where(lane == to, moved * (0.5 if r == 0 else 1.0), products)
                main_ref[BLOCKS - 1, 32 * half : 32 * (half + 1), :] = products.astype(BF16)
            for j, i in enumerate(SINGLES):
                main_ref[j, :32, :] = wide_ref[pl.ds(i, 32, stride=HALF), :].astype(BF16)
        else:
            places = [(j, 32, i) for j, i in enumerate(SINGLES)]
            places += [(len(SINGLES) + n, 32 * half, i) for n, pair in enumerate(PAIRS) for half, i in enumerate(pair)]
            for j, row, i in places:
                main_ref[j, row : row + 32, :] = wide_ref[pl.ds(i, 32, stride=HALF), :].astype(BF16)
    tails = [padded(source[BINS - 1].astype(F32), HALF, LANES) for source in (pair_ref, rime_ref)]
    grow = [padded(slim_ref[pl.ds(at, BINS, stride=2), :], HALF, LANES) for at in range(2)]
    for at, halves in enumerate((tails, grow)):
        rest_ref[at] = two_sided(jnp.concatenate(halves, axis=0)).astype(BF16)


def two_sided(block):
    half = block.shape[0] // 2
    empty = jnp.zeros((half, LANES), block.dtype)
    return jnp.concatenate(
        [
            jnp.concatenate([block[:half], empty], axis=1),
            jnp.concatenate([empty, block[half:]], axis=1),
        ],
        axis=0,
    )


def substep(round_ref, base_ref, state_ref, sat_ref, flag_ref, main_ref, rest_ref):
    steps = 2 * UNITS

    def place(step):
        block, first = step // 2, (step % 2) * 4
        return block, [(first + 2 * m, first + 2 * m + 1) for m in range(2)]

    def wide(ref, spot, rows, m):
        block, levels = spot
        return jnp.concatenate([ref[block, l, rows, :] for l in levels[m]], axis=1)

    def scoped(*accs):
        accs = (accs[: DEPTH + 3], accs[DEPTH + 3 :])

        def push(spot):
            for m in range(2):
                square = wide(round_ref, spot, slice(SQUARE[0], SQUARE[-1] + 1), m)
                operand = []
                for half, turns in enumerate(TURNS):
                    linear = wide(round_ref, spot, slice(HALF * half, HALF * (half + 1)), m)
                    pieces = [padded(linear, PRODUCTS, 2 * LANES)]
                    for r in turns:
                        other = pltpu.roll(square, len(SQUARE) - r, 0) if r else square
                        pieces.append((square * other)[: len(SQUARE) if 2 * r < len(SQUARE) else len(SQUARE) // 2])
                    operand.append(padded(jnp.concatenate(pieces, axis=0), LANES, 2 * LANES).astype(BF16))
                pltpu.matmul_push_rhs(jnp.concatenate(operand, axis=0), 0, m)

        def issue(j):
            if j >= BLOCKS:
                lhs = rest_ref[j - BLOCKS]
            elif j < len(SINGLES):
                lhs = two_sided(main_ref[j])
            elif j < BLOCKS - 1:
                lhs = jnp.concatenate([jnp.zeros((64, LANES), BF16), main_ref[j]], axis=1)
            else:
                lhs = jnp.concatenate([main_ref[j, :32, :], main_ref[j, 32:, :]], axis=1)
            for m in range(2):
                pltpu.matmul_acc_lhs(place_of(m, j), lhs, load_staged_rhs=0 if j == 0 else None)

        def place_of(m, j):
            return accs[m][j % DEPTH if j < BLOCKS - 1 else DEPTH + j - (BLOCKS - 1)]

        def body(step, carry):
            spot = place(step)
            block, levels = spot
            after = place(jnp.minimum(step + 1, steps - 1))
            sums = [[jnp.zeros((32, 2 * LANES), F32) for s in range(2)] for m in range(2)]
            for i in range(BLOCKS):
                if i == DEPTH - 1:
                    push(after)
                for m in range(2):
                    term = pltpu.matmul_pop(place_of(m, i))
                    if i < len(SINGLES):
                        by = wide(round_ref, spot, slice(SINGLES[i], SINGLES[i] + 1), m)
                        sums[m] = [sums[m][s] + term[32 * s : 32 * (s + 1)] * by for s in range(2)]
                    elif i < BLOCKS - 1:
                        for half, at in enumerate(PAIRS[i - len(SINGLES)]):
                            by = wide(round_ref, spot, slice(at, at + 1), m)
                            sums[m][1] = sums[m][1] + term[32 * half : 32 * (half + 1)] * by
                    else:
                        sums[m][0] = sums[m][0] + term
                if i + DEPTH < BLOCKS:
                    issue(i + DEPTH)
                else:
                    if i + DEPTH == BLOCKS:
                        issue(BLOCKS)
                        issue(BLOCKS + 1)
                    issue(i + DEPTH - BLOCKS)
            flag = flag_ref[block]
            flag = jnp.concatenate([flag, flag], axis=1)
            for m in range(2):
                last = pltpu.matmul_pop(place_of(m, BLOCKS))
                grow = pltpu.matmul_pop(place_of(m, BLOCKS + 1))
                liquid = wide(round_ref, spot, slice(0, HALF), m)
                for s in range(2):
                    tail = jnp.sum(last[HALF * s : HALF * (s + 1)] * liquid, axis=0, keepdims=True)
                    tail = padded(tail, 8, 2 * LANES)
                    gain = jnp.concatenate([sums[m][s], tail], axis=0) * flag
                    sat = jnp.concatenate([sat_ref[block, s * SLAB + l] for l in levels[m]], axis=1)
                    gain = gain + grow[HALF * s : HALF * (s + 1)] * sat
                    for half, l in enumerate(levels[m]):
                        rows = slice(HALF * s, HALF * (s + 1))
                        part = gain[:, half * LANES : (half + 1) * LANES]
                        state_ref[block, l, rows, :] = base_ref[block, l, rows, :] + part
            return carry

        push(place(0))
        for j in range(DEPTH):
            issue(j)
        lax.fori_loop(0, steps, body, 0)
        for j in range(DEPTH):
            for m in range(2):
                pltpu.matmul_pop(accs[m][j])

    pl.run_scoped(scoped, *accumulators())


def settle(state_ref, courant_ref, inverse_ref, lower_ref, flux_ref):
    def column(units, first, levels):
        flux = None
        for at in range(levels):
            u, l = units[at // SLAB], at % SLAB
            state = state_ref[u, l] if flux is None else state_ref[u, l] + flux
            settled = state * inverse_ref[first + at]
            state_ref[u, l] = settled
            flux = courant_ref[first + at] * settled
        return flux

    a = column((0, 1), 0, 2 * SLAB)
    b = column((2, 3), 0, 2 * SLAB)
    packed = column((4,), 2 * SLAB, SLAB)
    upper = turned(packed)
    for l in range(SLAB):
        state_ref[4, l] = state_ref[4, l] + lower_ref[l] * upper
    packed = packed + lower_ref[SLAB] * upper
    flux_ref[...] = flat_of(a, b, packed).astype(BF16)


def arrivals(prefix_ref, got_refs, weight_ref, at):
    flux = prefix_ref[...]
    for n, ref in enumerate(reversed(got_refs)):
        flux = flux + weight_ref[at + n] * ref[...].astype(F32)
    pieces = from_flat(flux)
    middle = pieces[4]
    other = turned(middle)
    left = on_left()
    packed = [jnp.where(left, other, middle), jnp.where(left, middle, other)]
    return tuple(jnp.concatenate(x, axis=0) for x in (pieces[0:2], pieces[2:4], packed))


def with_arrivals(state_ref, arrive_ref, fluxes, put):
    for u in range(UNITS):
        for l in range(SLAB):
            level = (l, SLAB + l, l, SLAB + l, 2 * SLAB + l)[u]
            put(u, l, state_ref[u, l] + arrive_ref[level] * fluxes[u // 2])


def table_kernel(
    index_ref, pair_ref, rime_ref, growth_ref, fall_ref, dens_ref,
    main_ref, rest_ref, courant_ref, inverse_ref, lower_ref,
    wide_ref, slim_ref,
):
    chip = index_ref[0] // 2
    courant = fall_column(fall_ref) * dens_ref[...]
    settle_tables(courant, chip, courant_ref, inverse_ref, lower_ref)
    pack_weights(pair_ref, rime_ref, growth_ref, wide_ref, slim_ref, main_ref, rest_ref)


def weight_kernel(index_ref, fall_ref, dens_ref, courant_ref, inverse_ref, flux_ref, arrive_ref, weight_ref, factor_ref):
    courant = fall_column(fall_ref) * dens_ref[...]
    arrive_table(courant_ref, inverse_ref, arrive_ref)
    scan_weights(courant, index_ref[0] // 2, factor_ref, weight_ref)


def load_kernel(
    index_ref, spectra_hbm, sat_hbm, flag_hbm, pair_hbm, rime_hbm, growth_hbm, fall_hbm, dens_hbm,
    sent_ref, own_ref, flag_ref, pair_ref, rime_ref, growth_ref, fall_ref, dens_ref,
    sems,
):
    core = index_ref[0] % 2
    pieces = []
    for at, ref in ((1 - core, sent_ref), (core, own_ref)):
        cols = pl.ds(pl.multiple_of(at * 2 * LANES, LANES), MINE)
        pieces.append((spectra_hbm.at[:, :, :, cols], ref.at[:, pl.ds(0, BINS)]))
        pieces.append((sat_hbm.at[:, :, cols], ref.at[:, BINS]))
    pieces += [(fall_hbm, fall_ref), (dens_hbm, dens_ref), (pair_hbm, pair_ref), (rime_hbm, rime_ref)]
    pieces += [(growth_hbm, growth_ref), (flag_hbm, flag_ref)]
    copies = [pltpu.make_async_copy(a, b, sems.at[n]) for n, (a, b) in enumerate(pieces)]
    for copy in copies:
        copy.start()
    for copy in copies:
        copy.wait()


def first_kernel(
    index_ref, own_ref, flag_row_ref, other_ref,
    main_ref, rest_ref, courant_ref, inverse_ref, lower_ref,
    state_ref, flux_ref, initial_ref, sat_ref, flag_ref,
):
    core = index_ref[0] % 2
    for u in range(UNITS):
        for l in range(SLAB):
            for s in range(2):
                row = u * SLAB * ROWS + ROWS * l + HALF * s + 32
                initial_ref[row : row + 8, :] = jnp.zeros((8, LANES), F32)
    a, b, middle = (pl.ds(pl.multiple_of(at * LANES, LANES), LANES) for at in (core, core + 1, 2 - 2 * core))
    first = core == 0
    own_half = on_left() == first

    def in_units(s, n):
        units = []
        for cols in (a, b):
            own, other = own_ref[s, n, :, cols].astype(F32), other_ref[s, n, :, cols].astype(F32)
            units += [jnp.where(first, own, other), jnp.where(first, other, own)]
        own, other = own_ref[s, n, :, middle].astype(F32), other_ref[s, n, :, middle].astype(F32)
        return units + [jnp.where(own_half, own, turned(other))]

    flags = (flag_row_ref[...] != 0).astype(F32)
    row_a, row_b = (jnp.where(first, flags[i : i + 1], flags[i + 3 : i + 4]) for i in range(2))
    flag_units = row_a, row_a, row_b, row_b, jnp.where(own_half, flags, turned(flags))[2:3]
    for u in range(UNITS):
        flag_ref[u] = flag_units[u]
    for s in range(2):
        units = in_units(s, BINS)
        for u in range(UNITS):
            for l in range(SLAB):
                sat_ref[u, s * SLAB + l] = units[u][l : l + 1]
        for n in range(BINS):
            units = in_units(s, n)
            for u in range(UNITS):
                initial_ref[pl.ds(u * SLAB * ROWS + HALF * s + n, SLAB, stride=ROWS), :] = units[u]
    initial = initial_ref.reshape(UNITS, SLAB, ROWS, LANES)
    substep(initial, initial, state_ref, sat_ref, flag_ref, main_ref, rest_ref)
    settle(state_ref, courant_ref, inverse_ref, lower_ref, flux_ref)


def second_kernel(
    state_in, prefix_ref, far_ref, near_ref, weight_ref, sat_ref, flag_ref, main_ref, rest_ref,
    courant_ref, inverse_ref, arrive_ref, lower_ref,
    state_ref, flux_ref,
    round_ref,
):
    def put(u, l, state):
        state_ref[u, l] = state
        round_ref[u, l] = state.astype(BF16).astype(F32)

    with_arrivals(state_in, arrive_ref, arrivals(prefix_ref, (far_ref, near_ref), weight_ref, 5), put)
    substep(round_ref, state_ref, state_ref, sat_ref, flag_ref, main_ref, rest_ref)
    settle(state_ref, courant_ref, inverse_ref, lower_ref, flux_ref)


def group_kernel(flux_ref, got1_ref, got2_ref, weight_ref, prefix_ref, send_ref):
    got1, got2 = got1_ref[...].astype(F32), got2_ref[...].astype(F32)
    prefix_ref[...] = weight_ref[0] * got1 + weight_ref[1] * got2
    total = weight_ref[2] * flux_ref[...].astype(F32) + weight_ref[3] * got1 + weight_ref[4] * got2
    send_ref[...] = total.astype(BF16)


def last_kernel(
    of_own, index_ref, state_ref, initial_ref, prefix_ref, farther_ref, far_ref, near_ref, weight_ref, arrive_ref,
    part_ref,
    change_ref,
):
    core = index_ref[0] % 2
    slab = core if of_own else 1 - core
    fluxes = arrivals(prefix_ref, (farther_ref, far_ref, near_ref), weight_ref, 5 + len(FIRST_SCAN[1]))
    for k in range(3):
        u = 2 * k + slab if k < 2 else 4
        for l in range(SLAB):
            level = SLAB * slab + l if k < 2 else 2 * SLAB + l
            row = u * SLAB * ROWS + ROWS * l
            state = state_ref[u, l] + arrive_ref[level] * fluxes[k]
            start = initial_ref[pl.ds(pl.multiple_of(row, 8), ROWS), :]
            change_ref[(k * SLAB + l) * ROWS : (k * SLAB + l + 1) * ROWS, :] = (state - start) * 0.5
    spots = [pl.ds(pl.multiple_of(at * LANES, LANES), LANES) for at in (core, core + 1, 2 - 2 * core)]
    for s in range(2):
        for n in range(BINS):
            for k in range(3):
                rows = change_ref[pl.ds(k * SLAB * ROWS + HALF * s + n, SLAB, stride=ROWS), :]
                if k == 2 and not of_own:
                    rows = turned(rows)
                part_ref[s, n, :, spots[k]] = rows.astype(BF16)


def merge_kernel(index_ref, keep_ref, got_ref, out_hbm, middle_ref, sems):
    core = index_ref[0] % 2

    def merge(left_ref, right_ref):
        parts = [
            (left_ref.at[:, :, :, pl.ds(0, 2 * LANES)], out_hbm.at[:, :, :, pl.ds(0, 2 * LANES)]),
            (right_ref.at[:, :, :, pl.ds(LANES, 2 * LANES)], out_hbm.at[:, :, :, pl.ds(3 * LANES, 2 * LANES)]),
            (middle_ref, out_hbm.at[:, :, :, pl.ds(2 * LANES, LANES)]),
        ]
        copies = [pltpu.make_async_copy(x, y, sems.at[n]) for n, (x, y) in enumerate(parts)]
        copies[0].start()
        copies[1].start()
        side = lax.broadcasted_iota(jnp.int32, (2, BINS, SLAB, LANES), 3) < LANES // 2
        middle_ref[...] = jnp.where(
            side, left_ref[:, :, :, 2 * LANES :].astype(F32), right_ref[:, :, :, :LANES].astype(F32)
        ).astype(BF16)
        copies[2].start()
        for copy in copies:
            copy.wait()

    @pl.when(core == 0)
    def _():
        merge(keep_ref, got_ref)

    @pl.when(core == 1)
    def _():
        merge(got_ref, keep_ref)


def accumulators():
    kinds = []
    for m in range(2):
        kinds += [pltpu.ACC(m)((rows, 2 * LANES), F32) for rows in (64,) * DEPTH + (32, ROWS, ROWS)]
    return kinds


def shaped(shape, dtype=F32):
    return jax.ShapeDtypeStruct(shape, dtype)


def local(spectra, supersat, cloud_flags, pair_kernel, rime_kernel, growth_matrix, fall_speed, density_factor):
    index = lax.axis_index("lat").astype(jnp.int32).reshape(1)
    swap = [(d, d ^ 1) for d in range(DEVS)]
    held = functools.partial(pltpu.with_memory_space_constraint, memory_space=pltpu.HBM)
    part = shaped((2, SENT, SLAB, MINE), BF16)
    tensor = shaped((BINS, BINS, BINS), BF16)
    sent, own, flag_rows, *parameters = pl.pallas_call(
        load_kernel,
        in_specs=[SMEM] + [HBM] * 8,
        out_specs=[VMEM] * 8,
        out_shape=[
            part,
            part,
            shaped((COLS // LANES, LANES), jnp.int32),
            tensor,
            tensor,
            shaped((BINS, 2, BINS), BF16),
            shaped((2, BINS)),
            shaped((1, LANES)),
        ],
        scratch_shapes=[pltpu.SemaphoreType.DMA((10,))],
        compiler_params=PARAMS,
        name="load_arguments",
    )(
        index, held(spectra), held(supersat), held(cloud_flags.reshape(COLS // LANES, LANES)), held(pair_kernel),
        held(rime_kernel), held(growth_matrix.transpose(1, 0, 2)), held(fall_speed), held(density_factor.reshape(1, LANES)),
    )
    other = lax.ppermute(sent, "lat", swap)

    state_shape = shaped((UNITS, SLAB, ROWS, LANES))
    flux_shape, flat_shape = shaped((FLAT, LANES), BF16), shaped((FLAT, LANES))
    level_shape = shaped((3 * SLAB, ROWS, LANES))
    cost = pl.CostEstimate(flops=2 * 2288 * 80 * SLAB * COLS, bytes_accessed=4_000_000, transcendentals=0)
    light = pl.CostEstimate(flops=1_000_000, bytes_accessed=8_000_000, transcendentals=0)

    main, rest, courant, inverse, lower = pl.pallas_call(
        table_kernel,
        in_specs=[SMEM] + [VMEM] * 5,
        out_specs=[VMEM] * 5,
        out_shape=[
            shaped((BLOCKS, 64, LANES), BF16),
            shaped((2, ROWS, 2 * LANES), BF16),
            level_shape,
            level_shape,
            shaped((SLAB + 1, ROWS, LANES)),
        ],
        scratch_shapes=[
            pltpu.VMEM((HALF * (BINS - 1), LANES), F32),
            pltpu.VMEM((2 * BINS, LANES), F32),
        ],
        compiler_params=PARAMS,
        cost_estimate=light,
        name="tables",
    )(index, *parameters)

    state, flux, initial, sat, flags = pl.pallas_call(
        first_kernel,
        in_specs=[SMEM] + [VMEM] * 8,
        out_specs=[VMEM] * 5,
        out_shape=[
            state_shape,
            flux_shape,
            shaped((UNITS * SLAB * ROWS, LANES)),
            shaped((UNITS, 2 * SLAB, 1, LANES)),
            shaped((UNITS, 1, LANES)),
        ],
        compiler_params=PARAMS,
        cost_estimate=cost,
        name="first_substep",
    )(index, own, flag_rows, other, main, rest, courant, inverse, lower)

    arrive, weight = pl.pallas_call(
        weight_kernel,
        in_specs=[SMEM] + [VMEM] * 4 + [pl.BlockSpec(memory_space=pl.ANY)],
        out_specs=[VMEM] * 2,
        out_shape=[level_shape, shaped((5 + len(SUMS), FLAT, LANES))],
        scratch_shapes=[pltpu.VMEM((CHIPS, ROWS, LANES), F32)],
        compiler_params=PARAMS,
        cost_estimate=light,
        name="scan_weights",
    )(index, *parameters[3:], courant, inverse, flux)

    def between(pairs):
        return [(2 * a + c, 2 * b + c) for a, b in pairs for c in range(2)]

    def scan(flux, plan):
        own, sums = plan
        got = [lax.ppermute(flux, "lat", between(pairs)) for pairs in own]
        prefix, send = pl.pallas_call(
            group_kernel,
            in_specs=[VMEM] * 4,
            out_specs=[VMEM] * 2,
            out_shape=[flat_shape, flux_shape],
            compiler_params=PARAMS,
            name="scan_group",
        )(flux, *got, weight)
        return prefix, *(lax.ppermute(send, "lat", between(pairs)) for pairs in reversed(sums))

    state, flux = pl.pallas_call(
        second_kernel,
        in_specs=[VMEM] * 13,
        out_specs=[VMEM] * 2,
        out_shape=[state_shape, flux_shape],
        scratch_shapes=[pltpu.VMEM((UNITS, SLAB, ROWS, LANES), F32)],
        compiler_params=PARAMS,
        cost_estimate=cost,
        name="second_substep",
    )(state, *scan(flux, FIRST_SCAN), weight, sat, flags, main, rest, courant, inverse, arrive, lower)

    arrived = scan(flux, LAST_SCAN)

    def tendencies(of_own, name):
        return pl.pallas_call(
            functools.partial(last_kernel, of_own),
            in_specs=[SMEM] + [VMEM] * 8,
            out_specs=VMEM,
            out_shape=shaped((2, BINS, SLAB, MINE), BF16),
            scratch_shapes=[pltpu.VMEM((3 * SLAB * ROWS, LANES), F32)],
            compiler_params=PARAMS,
            cost_estimate=light,
            name=name,
        )(index, state, initial, *arrived, weight, arrive)

    send = tendencies(False, "tendencies_sent")
    keep = tendencies(True, "tendencies_kept")

    got = lax.ppermute(send, "lat", swap)
    return pl.pallas_call(
        merge_kernel,
        in_specs=[SMEM] + [VMEM] * 2,
        out_specs=HBM,
        out_shape=shaped(spectra.shape, BF16),
        scratch_shapes=[pltpu.VMEM((2, BINS, SLAB, LANES), BF16), pltpu.SemaphoreType.DMA((3,))],
        compiler_params=PARAMS,
        cost_estimate=light,
        name="merge_slabs",
    )(index, keep, got)


def solution(mesh):
    return jax.shard_map(
        local,
        mesh=mesh,
        in_specs=(
            P(None, None, "lat", "lon"),
            P(None, "lat", "lon"),
            P("lon"),
            P(),
            P(),
            P(),
            P(),
            P(),
        ),
        out_specs=P(None, None, "lat", "lon"),
        check_vma=False,
    )
```

```python
import functools

import jax
import jax.numpy as jnp
from jax import lax
from jax.experimental import pallas as pl
from jax.experimental.pallas import tpu as pltpu
from jax.sharding import PartitionSpec as P

BINS = 33
HALF = 40
ROWS = 2 * HALF
SLAB = 8
COLS = 640
LANES = 128
MINE = 3 * LANES
SENT = BINS + 1
UNITS = 5
CHIPS = 8
GROUPS = ((0, 3), (3, 2), (5, 3))
FIRST_SCAN = (
    ([(0, 1), (1, 2), (2, 0), (3, 4), (4, 3), (5, 6), (6, 7)], [(0, 2), (1, 0), (2, 1), (5, 7)]),
    ([(1, 3), (2, 4), (3, 5), (0, 6), (4, 7)], [(0, 5), (4, 6), (1, 7)]),
)
LAST_SCAN = (
    ([(0, 1), (1, 2), (3, 4), (4, 3), (5, 6), (6, 7)], [(0, 2), (2, 1), (5, 7)]),
    ([(1, 3), (2, 4), (3, 5), (4, 6)], [(1, 7), (2, 5)], [(2, 6), (4, 7)]),
)
SUMS = FIRST_SCAN[1] + LAST_SCAN[1]
DEVS = 2 * CHIPS
FLAT = 168
DEPTH = 13
SQUARE = tuple(range(16, 32))
SINGLES = tuple(i for i in range(BINS) if i not in SQUARE)
PAIRS = tuple(zip(SQUARE[::2], SQUARE[1::2]))
BLOCKS = len(SINGLES) + len(PAIRS) + 1
PRODUCTS = 48
TURNS = (0, 1, 2, 3, 4), (5, 6, 7, 8)
F32 = jnp.float32
BF16 = jnp.bfloat16

VMEM = pl.BlockSpec(memory_space=pltpu.VMEM)
SMEM = pl.BlockSpec(memory_space=pltpu.SMEM)
HBM = pl.BlockSpec(memory_space=pltpu.HBM)
PARAMS = pltpu.CompilerParams(vmem_limit_bytes=24 * 1024 * 1024)


def on_left():
    return lax.broadcasted_iota(jnp.int32, (1, LANES), 1) < LANES // 2


def turned(value):
    return pltpu.roll(value, LANES // 2, 1)


def padded(value, rows, lanes):
    have_rows, have_lanes = value.shape
    if lanes > have_lanes:
        value = jnp.concatenate([value, jnp.zeros((have_rows, lanes - have_lanes), value.dtype)], axis=1)
    if rows > have_rows:
        value = jnp.concatenate([value, jnp.zeros((rows - have_rows, lanes), value.dtype)], axis=0)
    return value


def fall_column(fall_ref):
    row = lax.broadcasted_iota(jnp.int32, (HALF, BINS), 0)
    lane = lax.broadcasted_iota(jnp.int32, (HALF, BINS), 1)
    parts = []
    for s in range(2):
        spread = jnp.broadcast_to(fall_ref[s : s + 1, :], (HALF, BINS))
        parts.append(jnp.sum(jnp.where(row == lane, spread, 0.0), axis=1, keepdims=True))
    return jnp.concatenate(parts, axis=0)


def lane_of(value, lane):
    return jnp.broadcast_to(value[:, lane : lane + 1], (ROWS, LANES))


def settle_tables(courant, chip, courant_ref, inverse_ref, lower_ref):
    own = pltpu.roll(courant, lax.rem(LANES - 2 * SLAB * chip, LANES), 1)
    left = on_left()
    lower = None
    for l in range(2 * SLAB):
        here = lane_of(own, l)
        inverse = 1.0 / (1.0 + here)
        lower = None if l < SLAB else inverse if l == SLAB else lower * last * inverse
        last = here
        courant_ref[l] = here
        inverse_ref[l] = inverse
        if l >= SLAB:
            at = l - SLAB
            courant_ref[l + SLAB] = jnp.where(left, courant_ref[at], here)
            inverse_ref[l + SLAB] = jnp.where(left, inverse_ref[at], inverse)
            lower_ref[at] = jnp.where(left, 0.0, lower)
    lower_ref[SLAB] = jnp.where(left, 0.0, lower * last)


def arrive_table(courant_ref, inverse_ref, arrive_ref):
    left = on_left()
    arrive = inverse_ref[0]
    for l in range(2 * SLAB):
        if l > 0:
            arrive = arrive * courant_ref[l - 1] * inverse_ref[l]
        arrive_ref[l] = arrive
        if l >= SLAB:
            arrive_ref[l + SLAB] = jnp.where(left, arrive_ref[l - SLAB], arrive)


def flat_of(a, b, packed):
    middle = jnp.where(on_left(), turned(packed[HALF:]), packed[:HALF])
    pieces = (a[:HALF], a[HALF:], b[:HALF], b[HALF:], middle)
    row = lax.broadcasted_iota(jnp.int32, (8, LANES), 0)
    rest = jnp.zeros((8, LANES), F32)
    for at, piece in enumerate(pieces):
        tail = piece[32:]
        rest = jnp.where(row == at, tail if at == 0 else pltpu.roll(tail, at, 0), rest)
    return jnp.concatenate([piece[:32] for piece in pieces] + [rest], axis=0)


def from_flat(flat):
    row = lax.broadcasted_iota(jnp.int32, (8, LANES), 0)
    rest = flat[160:]
    pieces = []
    for at in range(5):
        tail = rest if at == 0 else pltpu.roll(rest, 8 - at, 0)
        pieces.append(jnp.concatenate([flat[32 * at : 32 * (at + 1)], jnp.where(row == 0, tail, 0.0)], axis=0))
    return pieces


def scan_weights(courant, chip, factor_ref, weight_ref):
    ratio = courant / (1.0 + courant)
    for step in (1, 2, 4, 8):
        ratio = ratio * pltpu.roll(ratio, LANES - step, 1)
    for e in range(CHIPS):
        factor_ref[e] = lane_of(ratio, 2 * SLAB * e)
    one = jnp.ones((ROWS, LANES), F32)

    def product(first, end):
        return lax.fori_loop(first, end, lambda e, w: w * factor_ref[e], one)

    first, size = jnp.int32(GROUPS[0][0]), jnp.int32(GROUPS[0][1])
    for start, count in GROUPS[1:]:
        first, size = jnp.where(chip >= start, start, first), jnp.where(chip >= start, count, size)
    place = chip - first
    for r in range(3):
        there = jnp.where(place >= r, place - r, place - r + size)
        fits = there >= 0
        if r > 0:
            w = jnp.where(fits & (there < place), product(first + there + 1, chip), 0.0)
            weight_ref[r - 1] = flat_of(w, w, w)
        w = jnp.where(fits, product(first + there + 1, first + size), 0.0)
        weight_ref[2 + r] = flat_of(w, w, w)
    into = []
    for start, _ in GROUPS[1:]:
        w = jnp.where(chip >= start, product(start, chip), 0.0)
        into.append(flat_of(w, w, w))
    for n, pairs in enumerate(SUMS):
        of_first = functools.reduce(jnp.logical_or, [chip == b for a, b in pairs if a < GROUPS[1][0]], False)
        weight_ref[5 + n] = jnp.where(of_first, into[0], into[1])


def pack_weights(pair_ref, rime_ref, growth_ref, wide_ref, slim_ref, main_ref, rest_ref):
    for k in range(BINS):
        slim_ref[2 * k : 2 * k + 2, :] = padded(growth_ref[k].astype(F32), 2, LANES)
    low, size = SQUARE[0], len(SQUARE)
    lane = lax.broadcasted_iota(jnp.int32, (1, LANES), 1)
    in_square = (lane >= low) & (lane < low + size)
    for at, source in ((0, pair_ref), (1, rime_ref)):
        for k in range(BINS - 1):
            wide_ref[HALF * k : HALF * (k + 1), :] = padded(source[k].astype(F32), HALF, LANES)
        if at == 0:
            for first in range(0, BINS - 1, LANES // size):
                ks = range(first, min(first + LANES // size, BINS - 1))
                turn = jnp.concatenate([wide_ref[HALF * k + low : HALF * k + low + size, :] for k in ks], axis=0).T
                for n, k in enumerate(ks):
                    shift = (low - size * n) % LANES
                    extra = pltpu.roll(turn[:HALF], shift, 1) if shift else turn[:HALF]
                    rows = slice(HALF * k, HALF * (k + 1))
                    wide_ref[rows, :] = wide_ref[rows, :] + jnp.where(in_square, extra, 0.0)
            for half, turns in enumerate(TURNS):
                products = jnp.zeros((32, LANES), F32)
                for i in range(size):
                    rows = wide_ref[pl.ds(low + i, 32, stride=HALF), :]
                    for n, r in enumerate(turns):
                        if 2 * r < size or i < size // 2:
                            to, there = PRODUCTS + size * n + i, low + (i + r) % size
                            moved = pltpu.roll(rows, (to - there) % LANES, 1) if to != there else rows
                            products = jnp.where(lane == to, moved * (0.5 if r == 0 else 1.0), products)
                main_ref[BLOCKS - 1, 32 * half : 32 * (half + 1), :] = products.astype(BF16)
            for j, i in enumerate(SINGLES):
                main_ref[j, :32, :] = wide_ref[pl.ds(i, 32, stride=HALF), :].astype(BF16)
        else:
            places = [(j, 32, i) for j, i in enumerate(SINGLES)]
            places += [(len(SINGLES) + n, 32 * half, i) for n, pair in enumerate(PAIRS) for half, i in enumerate(pair)]
            for j, row, i in places:
                main_ref[j, row : row + 32, :] = wide_ref[pl.ds(i, 32, stride=HALF), :].astype(BF16)
    tails = [padded(source[BINS - 1].astype(F32), HALF, LANES) for source in (pair_ref, rime_ref)]
    grow = [padded(slim_ref[pl.ds(at, BINS, stride=2), :], HALF, LANES) for at in range(2)]
    for at, halves in enumerate((tails, grow)):
        rest_ref[at] = two_sided(jnp.concatenate(halves, axis=0)).astype(BF16)


def two_sided(block):
    half = block.shape[0] // 2
    empty = jnp.zeros((half, LANES), block.dtype)
    return jnp.concatenate(
        [
            jnp.concatenate([block[:half], empty], axis=1),
            jnp.concatenate([empty, block[half:]], axis=1),
        ],
        axis=0,
    )


def substep(base_ref, state_ref, sat_ref, flag_ref, main_ref, rest_ref):
    steps = 2 * UNITS

    def place(step):
        block, first = step // 2, (step % 2) * 4
        return block, [(first + 2 * m, first + 2 * m + 1) for m in range(2)]

    def wide(spot, rows, m):
        block, levels = spot
        return jnp.concatenate([base_ref[block, l, rows, :] for l in levels[m]], axis=1).astype(BF16).astype(F32)

    def scoped(*accs):
        accs = (accs[: DEPTH + 3], accs[DEPTH + 3 :])

        def push(spot):
            for m in range(2):
                square = wide(spot, slice(SQUARE[0], SQUARE[-1] + 1), m)
                operand = []
                for half, turns in enumerate(TURNS):
                    linear = wide(spot, slice(HALF * half, HALF * (half + 1)), m)
                    pieces = [padded(linear, PRODUCTS, 2 * LANES)]
                    for r in turns:
                        other = pltpu.roll(square, len(SQUARE) - r, 0) if r else square
                        pieces.append((square * other)[: len(SQUARE) if 2 * r < len(SQUARE) else len(SQUARE) // 2])
                    operand.append(padded(jnp.concatenate(pieces, axis=0), LANES, 2 * LANES).astype(BF16))
                pltpu.matmul_push_rhs(jnp.concatenate(operand, axis=0), 0, m)

        def issue(j):
            if j >= BLOCKS:
                lhs = rest_ref[j - BLOCKS]
            elif j < len(SINGLES):
                lhs = two_sided(main_ref[j])
            elif j < BLOCKS - 1:
                lhs = jnp.concatenate([jnp.zeros((64, LANES), BF16), main_ref[j]], axis=1)
            else:
                lhs = jnp.concatenate([main_ref[j, :32, :], main_ref[j, 32:, :]], axis=1)
            for m in range(2):
                pltpu.matmul_acc_lhs(place_of(m, j), lhs, load_staged_rhs=0 if j == 0 else None)

        def place_of(m, j):
            return accs[m][j % DEPTH if j < BLOCKS - 1 else DEPTH + j - (BLOCKS - 1)]

        def body(step, carry):
            spot = place(step)
            block, levels = spot
            after = place(jnp.minimum(step + 1, steps - 1))
            sums = [[jnp.zeros((32, 2 * LANES), F32) for s in range(2)] for m in range(2)]
            for i in range(BLOCKS):
                if i == DEPTH - 1:
                    push(after)
                for m in range(2):
                    term = pltpu.matmul_pop(place_of(m, i))
                    if i < len(SINGLES):
                        by = wide(spot, slice(SINGLES[i], SINGLES[i] + 1), m)
                        sums[m] = [sums[m][s] + term[32 * s : 32 * (s + 1)] * by for s in range(2)]
                    elif i < BLOCKS - 1:
                        for half, at in enumerate(PAIRS[i - len(SINGLES)]):
                            by = wide(spot, slice(at, at + 1), m)
                            sums[m][1] = sums[m][1] + term[32 * half : 32 * (half + 1)] * by
                    else:
                        sums[m][0] = sums[m][0] + term
                if i + DEPTH < BLOCKS:
                    issue(i + DEPTH)
                else:
                    if i + DEPTH == BLOCKS:
                        issue(BLOCKS)
                        issue(BLOCKS + 1)
                    issue(i + DEPTH - BLOCKS)
            flag = flag_ref[block]
            flag = jnp.concatenate([flag, flag], axis=1)
            for m in range(2):
                last = pltpu.matmul_pop(place_of(m, BLOCKS))
                grow = pltpu.matmul_pop(place_of(m, BLOCKS + 1))
                liquid = wide(spot, slice(0, HALF), m)
                for s in range(2):
                    tail = jnp.sum(last[HALF * s : HALF * (s + 1)] * liquid, axis=0, keepdims=True)
                    tail = padded(tail, 8, 2 * LANES)
                    gain = jnp.concatenate([sums[m][s], tail], axis=0) * flag
                    sat = jnp.concatenate([sat_ref[block, s * SLAB + l] for l in levels[m]], axis=1)
                    gain = gain + grow[HALF * s : HALF * (s + 1)] * sat
                    for half, l in enumerate(levels[m]):
                        rows = slice(HALF * s, HALF * (s + 1))
                        part = gain[:, half * LANES : (half + 1) * LANES]
                        state_ref[block, l, rows, :] = base_ref[block, l, rows, :] + part
            return carry

        push(place(0))
        for j in range(DEPTH):
            issue(j)
        lax.fori_loop(0, steps, body, 0)
        for j in range(DEPTH):
            for m in range(2):
                pltpu.matmul_pop(accs[m][j])

    pl.run_scoped(scoped, *accumulators())


def settle(state_ref, courant_ref, inverse_ref, lower_ref, flux_ref):
    def column(units, first, levels):
        flux = None
        for at in range(levels):
            u, l = units[at // SLAB], at % SLAB
            state = state_ref[u, l] if flux is None else state_ref[u, l] + flux
            settled = state * inverse_ref[first + at]
            state_ref[u, l] = settled
            flux = courant_ref[first + at] * settled
        return flux

    a = column((0, 1), 0, 2 * SLAB)
    b = column((2, 3), 0, 2 * SLAB)
    packed = column((4,), 2 * SLAB, SLAB)
    upper = turned(packed)
    for l in range(SLAB):
        state_ref[4, l] = state_ref[4, l] + lower_ref[l] * upper
    packed = packed + lower_ref[SLAB] * upper
    flux_ref[...] = flat_of(a, b, packed).astype(BF16)


def arrivals(prefix_ref, got_refs, weight_ref, at):
    flux = prefix_ref[...]
    for n, ref in enumerate(reversed(got_refs)):
        flux = flux + weight_ref[at + n] * ref[...].astype(F32)
    pieces = from_flat(flux)
    middle = pieces[4]
    other = turned(middle)
    left = on_left()
    packed = [jnp.where(left, other, middle), jnp.where(left, middle, other)]
    return tuple(jnp.concatenate(x, axis=0) for x in (pieces[0:2], pieces[2:4], packed))


def with_arrivals(state_ref, arrive_ref, fluxes, put):
    for u in range(UNITS):
        for l in range(SLAB):
            level = (l, SLAB + l, l, SLAB + l, 2 * SLAB + l)[u]
            put(u, l, state_ref[u, l] + arrive_ref[level] * fluxes[u // 2])


def table_kernel(
    index_ref, pair_ref, rime_ref, growth_ref, fall_ref, dens_ref,
    main_ref, rest_ref, courant_ref, inverse_ref, lower_ref,
    wide_ref, slim_ref,
):
    chip = index_ref[0] // 2
    courant = fall_column(fall_ref) * dens_ref[...]
    settle_tables(courant, chip, courant_ref, inverse_ref, lower_ref)
    pack_weights(pair_ref, rime_ref, growth_ref, wide_ref, slim_ref, main_ref, rest_ref)


def weight_kernel(index_ref, fall_ref, dens_ref, courant_ref, inverse_ref, flux_ref, arrive_ref, weight_ref, factor_ref):
    courant = fall_column(fall_ref) * dens_ref[...]
    arrive_table(courant_ref, inverse_ref, arrive_ref)
    scan_weights(courant, index_ref[0] // 2, factor_ref, weight_ref)


def load_kernel(
    index_ref, spectra_hbm, sat_hbm, flag_hbm, pair_hbm, rime_hbm, growth_hbm, fall_hbm, dens_hbm,
    sent_ref, own_ref, flag_ref, pair_ref, rime_ref, growth_ref, fall_ref, dens_ref,
    sems,
):
    core = index_ref[0] % 2
    pieces = []
    for at, ref in ((1 - core, sent_ref), (core, own_ref)):
        cols = pl.ds(pl.multiple_of(at * 2 * LANES, LANES), MINE)
        pieces.append((spectra_hbm.at[:, :, :, cols], ref.at[:, pl.ds(0, BINS)]))
        pieces.append((sat_hbm.at[:, :, cols], ref.at[:, BINS]))
    pieces += [(fall_hbm, fall_ref), (dens_hbm, dens_ref), (pair_hbm, pair_ref), (rime_hbm, rime_ref)]
    pieces += [(growth_hbm, growth_ref), (flag_hbm, flag_ref)]
    copies = [pltpu.make_async_copy(a, b, sems.at[n]) for n, (a, b) in enumerate(pieces)]
    for copy in copies:
        copy.start()
    for copy in copies:
        copy.wait()


def first_kernel(
    index_ref, own_ref, flag_row_ref, other_ref,
    main_ref, rest_ref, courant_ref, inverse_ref, lower_ref,
    state_ref, flux_ref, initial_ref, sat_ref, flag_ref,
):
    core = index_ref[0] % 2
    for u in range(UNITS):
        for l in range(SLAB):
            for s in range(2):
                row = u * SLAB * ROWS + ROWS * l + HALF * s + 32
                initial_ref[row : row + 8, :] = jnp.zeros((8, LANES), F32)
    a, b, middle = (pl.ds(pl.multiple_of(at * LANES, LANES), LANES) for at in (core, core + 1, 2 - 2 * core))
    first = core == 0
    own_half = on_left() == first

    def in_units(s, n):
        units = []
        for cols in (a, b):
            own, other = own_ref[s, n, :, cols].astype(F32), other_ref[s, n, :, cols].astype(F32)
            units += [jnp.where(first, own, other), jnp.where(first, other, own)]
        own, other = own_ref[s, n, :, middle].astype(F32), other_ref[s, n, :, middle].astype(F32)
        return units + [jnp.where(own_half, own, turned(other))]

    flags = (flag_row_ref[...] != 0).astype(F32)
    row_a, row_b = (jnp.where(first, flags[i : i + 1], flags[i + 3 : i + 4]) for i in range(2))
    flag_units = row_a, row_a, row_b, row_b, jnp.where(own_half, flags, turned(flags))[2:3]
    for u in range(UNITS):
        flag_ref[u] = flag_units[u]
    for s in range(2):
        units = in_units(s, BINS)
        for u in range(UNITS):
            for l in range(SLAB):
                sat_ref[u, s * SLAB + l] = units[u][l : l + 1]
        for n in range(BINS):
            units = in_units(s, n)
            for u in range(UNITS):
                initial_ref[pl.ds(u * SLAB * ROWS + HALF * s + n, SLAB, stride=ROWS), :] = units[u]
    initial = initial_ref.reshape(UNITS, SLAB, ROWS, LANES)
    substep(initial, state_ref, sat_ref, flag_ref, main_ref, rest_ref)
    settle(state_ref, courant_ref, inverse_ref, lower_ref, flux_ref)


def second_kernel(
    state_in, prefix_ref, far_ref, near_ref, weight_ref, sat_ref, flag_ref, main_ref, rest_ref,
    courant_ref, inverse_ref, arrive_ref, lower_ref,
    state_ref, flux_ref,
):
    def put(u, l, state):
        state_ref[u, l] = state

    with_arrivals(state_in, arrive_ref, arrivals(prefix_ref, (far_ref, near_ref), weight_ref, 5), put)
    substep(state_ref, state_ref, sat_ref, flag_ref, main_ref, rest_ref)
    settle(state_ref, courant_ref, inverse_ref, lower_ref, flux_ref)


def group_kernel(flux_ref, got1_ref, got2_ref, weight_ref, prefix_ref, send_ref):
    got1, got2 = got1_ref[...].astype(F32), got2_ref[...].astype(F32)
    prefix_ref[...] = weight_ref[0] * got1 + weight_ref[1] * got2
    total = weight_ref[2] * flux_ref[...].astype(F32) + weight_ref[3] * got1 + weight_ref[4] * got2
    send_ref[...] = total.astype(BF16)


def last_kernel(
    of_own, index_ref, state_ref, initial_ref, prefix_ref, farther_ref, far_ref, near_ref, weight_ref, arrive_ref,
    part_ref,
    change_ref,
):
    core = index_ref[0] % 2
    slab = core if of_own else 1 - core
    fluxes = arrivals(prefix_ref, (farther_ref, far_ref, near_ref), weight_ref, 5 + len(FIRST_SCAN[1]))
    for k in range(3):
        u = 2 * k + slab if k < 2 else 4
        for l in range(SLAB):
            level = SLAB * slab + l if k < 2 else 2 * SLAB + l
            row = u * SLAB * ROWS + ROWS * l
            state = state_ref[u, l] + arrive_ref[level] * fluxes[k]
            start = initial_ref[pl.ds(pl.multiple_of(row, 8), ROWS), :]
            change_ref[(k * SLAB + l) * ROWS : (k * SLAB + l + 1) * ROWS, :] = (state - start) * 0.5
    spots = [pl.ds(pl.multiple_of(at * LANES, LANES), LANES) for at in (core, core + 1, 2 - 2 * core)]
    for s in range(2):
        for n in range(BINS):
            for k in range(3):
                rows = change_ref[pl.ds(k * SLAB * ROWS + HALF * s + n, SLAB, stride=ROWS), :]
                if k == 2 and not of_own:
                    rows = turned(rows)
                part_ref[s, n, :, spots[k]] = rows.astype(BF16)


def merge_kernel(index_ref, keep_ref, got_ref, out_hbm, middle_ref, sems):
    core = index_ref[0] % 2

    def merge(left_ref, right_ref):
        parts = [
            (left_ref.at[:, :, :, pl.ds(0, 2 * LANES)], out_hbm.at[:, :, :, pl.ds(0, 2 * LANES)]),
            (right_ref.at[:, :, :, pl.ds(LANES, 2 * LANES)], out_hbm.at[:, :, :, pl.ds(3 * LANES, 2 * LANES)]),
            (middle_ref, out_hbm.at[:, :, :, pl.ds(2 * LANES, LANES)]),
        ]
        copies = [pltpu.make_async_copy(x, y, sems.at[n]) for n, (x, y) in enumerate(parts)]
        copies[0].start()
        copies[1].start()
        side = lax.broadcasted_iota(jnp.int32, (2, BINS, SLAB, LANES), 3) < LANES // 2
        middle_ref[...] = jnp.where(
            side, left_ref[:, :, :, 2 * LANES :].astype(F32), right_ref[:, :, :, :LANES].astype(F32)
        ).astype(BF16)
        copies[2].start()
        for copy in copies:
            copy.wait()

    @pl.when(core == 0)
    def _():
        merge(keep_ref, got_ref)

    @pl.when(core == 1)
    def _():
        merge(got_ref, keep_ref)


def accumulators():
    kinds = []
    for m in range(2):
        kinds += [pltpu.ACC(m)((rows, 2 * LANES), F32) for rows in (64,) * DEPTH + (32, ROWS, ROWS)]
    return kinds


def shaped(shape, dtype=F32):
    return jax.ShapeDtypeStruct(shape, dtype)


def local(spectra, supersat, cloud_flags, pair_kernel, rime_kernel, growth_matrix, fall_speed, density_factor):
    index = lax.axis_index("lat").astype(jnp.int32).reshape(1)
    swap = [(d, d ^ 1) for d in range(DEVS)]
    held = functools.partial(pltpu.with_memory_space_constraint, memory_space=pltpu.HBM)
    part = shaped((2, SENT, SLAB, MINE), BF16)
    tensor = shaped((BINS, BINS, BINS), BF16)
    sent, own, flag_rows, *parameters = pl.pallas_call(
        load_kernel,
        in_specs=[SMEM] + [HBM] * 8,
        out_specs=[VMEM] * 8,
        out_shape=[
            part,
            part,
            shaped((COLS // LANES, LANES), jnp.int32),
            tensor,
            tensor,
            shaped((BINS, 2, BINS), BF16),
            shaped((2, BINS)),
            shaped((1, LANES)),
        ],
        scratch_shapes=[pltpu.SemaphoreType.DMA((10,))],
        compiler_params=PARAMS,
        name="load_arguments",
    )(
        index, held(spectra), held(supersat), held(cloud_flags.reshape(COLS // LANES, LANES)), held(pair_kernel),
        held(rime_kernel), held(growth_matrix.transpose(1, 0, 2)), held(fall_speed), held(density_factor.reshape(1, LANES)),
    )
    other = lax.ppermute(sent, "lat", swap)

    state_shape = shaped((UNITS, SLAB, ROWS, LANES))
    flux_shape, flat_shape = shaped((FLAT, LANES), BF16), shaped((FLAT, LANES))
    level_shape = shaped((3 * SLAB, ROWS, LANES))
    cost = pl.CostEstimate(flops=2 * 2288 * 80 * SLAB * COLS, bytes_accessed=4_000_000, transcendentals=0)
    light = pl.CostEstimate(flops=1_000_000, bytes_accessed=8_000_000, transcendentals=0)

    main, rest, courant, inverse, lower = pl.pallas_call(
        table_kernel,
        in_specs=[SMEM] + [VMEM] * 5,
        out_specs=[VMEM] * 5,
        out_shape=[
            shaped((BLOCKS, 64, LANES), BF16),
            shaped((2, ROWS, 2 * LANES), BF16),
            level_shape,
            level_shape,
            shaped((SLAB + 1, ROWS, LANES)),
        ],
        scratch_shapes=[
            pltpu.VMEM((HALF * (BINS - 1), LANES), F32),
            pltpu.VMEM((2 * BINS, LANES), F32),
        ],
        compiler_params=PARAMS,
        cost_estimate=light,
        name="tables",
    )(index, *parameters)

    state, flux, initial, sat, flags = pl.pallas_call(
        first_kernel,
        in_specs=[SMEM] + [VMEM] * 8,
        out_specs=[VMEM] * 5,
        out_shape=[
            state_shape,
            flux_shape,
            shaped((UNITS * SLAB * ROWS, LANES)),
            shaped((UNITS, 2 * SLAB, 1, LANES)),
            shaped((UNITS, 1, LANES)),
        ],
        compiler_params=PARAMS,
        cost_estimate=cost,
        name="first_substep",
    )(index, own, flag_rows, other, main, rest, courant, inverse, lower)

    arrive, weight = pl.pallas_call(
        weight_kernel,
        in_specs=[SMEM] + [VMEM] * 4 + [pl.BlockSpec(memory_space=pl.ANY)],
        out_specs=[VMEM] * 2,
        out_shape=[level_shape, shaped((5 + len(SUMS), FLAT, LANES))],
        scratch_shapes=[pltpu.VMEM((CHIPS, ROWS, LANES), F32)],
        compiler_params=PARAMS,
        cost_estimate=light,
        name="scan_weights",
    )(index, *parameters[3:], courant, inverse, flux)

    def between(pairs):
        return [(2 * a + c, 2 * b + c) for a, b in pairs for c in range(2)]

    def scan(flux, plan):
        own, sums = plan
        got = [lax.ppermute(flux, "lat", between(pairs)) for pairs in own]
        prefix, send = pl.pallas_call(
            group_kernel,
            in_specs=[VMEM] * 4,
            out_specs=[VMEM] * 2,
            out_shape=[flat_shape, flux_shape],
            compiler_params=PARAMS,
            name="scan_group",
        )(flux, *got, weight)
        return prefix, *(lax.ppermute(send, "lat", between(pairs)) for pairs in reversed(sums))

    state, flux = pl.pallas_call(
        second_kernel,
        in_specs=[VMEM] * 13,
        out_specs=[VMEM] * 2,
        out_shape=[state_shape, flux_shape],
        compiler_params=PARAMS,
        cost_estimate=cost,
        name="second_substep",
    )(state, *scan(flux, FIRST_SCAN), weight, sat, flags, main, rest, courant, inverse, arrive, lower)

    arrived = scan(flux, LAST_SCAN)

    def tendencies(of_own, name):
        return pl.pallas_call(
            functools.partial(last_kernel, of_own),
            in_specs=[SMEM] + [VMEM] * 8,
            out_specs=VMEM,
            out_shape=shaped((2, BINS, SLAB, MINE), BF16),
            scratch_shapes=[pltpu.VMEM((3 * SLAB * ROWS, LANES), F32)],
            compiler_params=PARAMS,
            cost_estimate=light,
            name=name,
        )(index, state, initial, *arrived, weight, arrive)

    send = tendencies(False, "tendencies_sent")
    keep = tendencies(True, "tendencies_kept")

    got = lax.ppermute(send, "lat", swap)
    return pl.pallas_call(
        merge_kernel,
        in_specs=[SMEM] + [VMEM] * 2,
        out_specs=HBM,
        out_shape=shaped(spectra.shape, BF16),
        scratch_shapes=[pltpu.VMEM((2, BINS, SLAB, LANES), BF16), pltpu.SemaphoreType.DMA((3,))],
        compiler_params=PARAMS,
        cost_estimate=light,
        name="merge_slabs",
    )(index, keep, got)


def solution(mesh):
    return jax.shard_map(
        local,
        mesh=mesh,
        in_specs=(
            P(None, None, "lat", "lon"),
            P(None, "lat", "lon"),
            P("lon"),
            P(),
            P(),
            P(),
            P(),
            P(),
        ),
        out_specs=P(None, None, "lat", "lon"),
        check_vma=False,
    )
```
